32 devices in a mesh: atm: 8 (over z, x), ocn: 4 (over y, core).
Axes of the slice: x: 2, y: 2, z: 4, core: 2. Of those that a mesh axis runs over, the one named last changes fastest.
Arguments:
- atm_state: float32 [3, 63, 65536], P(None, None, ('atm', 'ocn')), may hold values from -6 to 6
- diffusivity: float32 [62, 65536], P(None, ('atm', 'ocn')), may hold values from 0.1 to 10
- send_slot: int32 [32, 64], P(('atm', 'ocn')), may hold values from 0 to 127, as said below
- atm_block: int32 [32, 64], P(('atm', 'ocn')), may hold values from 0 to 15
- recv_row: int32 [32, 128], P(('atm', 'ocn')), may hold values from -1 to 31, as said below
- remap_weight: bfloat16 [2048, 128, 128], P(('atm', 'ocn')), may hold values from 0 to 0.0078125
- ocean_tracer: float32 [3, 75, 256, 512], P(None, None, 'atm', 'ocn'), may hold values from -6 to 6
- ocean_velocity: float32 [2, 75, 256, 512], P(None, None, 'atm', 'ocn'), may hold values from -0.24 to 0.24
- exchange_coef: float32 [256, 512], P('atm', 'ocn'), may hold values from 0.2 to 5
- surface_kind: int32 [256, 512], P('atm', 'ocn'), may hold values from 0 to 2
- ice_surface: float32 [3, 256, 512], P(None, 'atm', 'ocn'), may hold values from -6 to 6
Outputs:
- atm_new: float32 [3, 63, 65536], P(None, None, ('atm', 'ocn'))
- ocean_new: float32 [3, 75, 256, 512], P(None, None, 'atm', 'ocn')
The draws below stay inside these ranges and needn't reach their ends.
Inputs may be any that keep to these rules, and one draw needn't show every extreme that they name: `send_slot`: entry [s, b] = d * 4 + k names owner d and slot k for block b of device s; entries of a row are distinct. Each device sends 4 blocks to itself, and one owner receives 4 blocks from every device. `recv_row`: entry [d, s * 4 + k] is the row of owner d's tile that receives the block that device s sends to slot k of d, and -1 exactly where device s sends nothing to that slot.
All inputs are finite; a program needn't handle non-finite values.
Results may differ from the reference program's by a relative error of at most 0.0003.
Values may be sent and summed in bfloat16 or wider, within the bound.
No kernel may reach another device: no remote copies, remote signals or barrier semaphores. Data moves between devices by JAX's collectives and lax.ppermute only.
A program may use at most 192 MiB of HBM per device.

```python
import math
import jax
import jax.numpy as jnp
from jax import lax

NV = 3
LEV = 63
OLEV = 75
ORX = 128
CAP = 4
NSUB = 4
ORY = 32
NBLK = 64
ABLK = 16
COLUMNS = 65536
NY_O = 256
NX_O = 512
N_OCN = 4
DEVICES = 32


def routing_table(key):
    base = jax.random.fold_in(key, 9173)
    key_hot, key_score, key_rows = jax.random.split(base, 3)
    slot_count = DEVICES * CAP
    slot_ids = jnp.arange(slot_count, dtype=jnp.int32)
    owners = slot_ids // CAP
    sources = jnp.arange(DEVICES, dtype=jnp.int32)[:, None]
    hottest = jax.random.randint(key_hot, (), 0, DEVICES, dtype=jnp.int32)
    noise_bits = jax.random.randint(key_score, (DEVICES, slot_count), 0, 2 ** 29 // slot_count, dtype=jnp.int32)
    scores = noise_bits * slot_count + slot_ids[None, :]
    scores = jnp.where(owners[None, :] == hottest, 2 ** 29 + slot_ids[None, :], scores)
    scores = jnp.where(owners[None, :] == sources, 2 ** 30 + slot_ids[None, :], scores)
    top_values, top_index = lax.top_k(scores, NBLK)
    occupied = scores >= top_values[:, -1:]
    rows_drawn = jax.random.randint(key_rows, (DEVICES, DEVICES, CAP), 0, ORY, dtype=jnp.int32)
    balanced = (jnp.arange(DEVICES, dtype=jnp.int32)[:, None] * CAP + jnp.arange(CAP, dtype=jnp.int32)[None, :]) % ORY
    is_hot = jnp.arange(DEVICES, dtype=jnp.int32)[:, None, None] == hottest
    rows_drawn = jnp.where(is_hot, balanced[None], rows_drawn)
    is_live = occupied.reshape(DEVICES, DEVICES, CAP).transpose(1, 0, 2)
    received = jnp.where(is_live, rows_drawn, -1).reshape(DEVICES, slot_count)
    return (top_index.astype(jnp.int32), received.astype(jnp.int32))


def draw_send_slot(key, part):
    return routing_table(key)[0]


def draw_recv_row(key, part):
    return routing_table(key)[1]


def set_ends(drawn, key, low, largest):
    dims = drawn.shape
    index_at = [jax.random.randint(jax.random.fold_in(key, axis), (), 0, dims[axis]) for axis in range(len(dims))]
    drawn = drawn.at[tuple(index_at)].set(low)
    longest = dims.index(max(dims))
    index_at[longest] = (index_at[longest] + 1) % dims[longest]
    return drawn.at[tuple(index_at)].set(largest)


def block_scale(rng, shape, shards, least, largest):
    loudness, own = 1.0, jax.random.fold_in(rng, 6)
    for axis_at, blocks in shards:
        draws = jnp.exp(jax.random.uniform(jax.random.fold_in(own, axis_at), (blocks,), jnp.float32, least / len(shards), largest / len(shards)))
        loudness = loudness * jnp.repeat(draws, shape[axis_at] // blocks).reshape([-1 if axis == axis_at else 1 for axis in range(len(shape))])
    return loudness


def gaussian(own_key, extent, deviation, limit, cuts=(), held_as=jnp.bfloat16):
    values = jax.random.normal(own_key, extent, jnp.float32) * deviation
    if len(cuts) > 0:
        values = block_scale(own_key, extent, cuts, -0.22, 0.18) * values
    return jnp.clip(values, min=-limit, max=limit).astype(held_as)


def setup_inputs(seed: int = 0) -> dict:
    arg_keys = jax.random.split(jax.random.key(seed), 12)
    return {
        "atm_state": gaussian(arg_keys[0], (NV, LEV, COLUMNS), 1.0, 6.0, ((2, 32),), jnp.float32),
        "diffusivity": jnp.clip(jnp.exp(math.log(10.0) - 4.6051702 * jax.random.uniform(arg_keys[1], (LEV - 1, COLUMNS), jnp.float32) ** block_scale(arg_keys[1], (LEV - 1, COLUMNS), ((1, 32),), -0.2, 0.2)), 0.1, 10.0),
        "send_slot": draw_send_slot(jax.random.fold_in(arg_keys[11], 71), 0),
        "atm_block": set_ends(jax.random.randint(arg_keys[3], (DEVICES, NBLK), 0, ABLK), jax.random.fold_in(arg_keys[3], 1), 0, ABLK - 1).astype(jnp.int32),
        "recv_row": draw_recv_row(jax.random.fold_in(arg_keys[11], 71), 0),
        "remap_weight": jnp.clip(0.0078125 * jax.random.uniform(arg_keys[5], (DEVICES * NBLK, ORX, ORX), jnp.float32) ** block_scale(arg_keys[5], (DEVICES * NBLK, ORX, ORX), ((0, 32),), -0.2, 0.2), 0.0, 0.0078125).astype(jnp.bfloat16),
        "ocean_tracer": gaussian(arg_keys[6], (NV, OLEV, NY_O, NX_O), 1.0, 6.0, ((2, 8), (3, 4)), jnp.float32),
        "ocean_velocity": jnp.clip(jax.random.uniform(arg_keys[7], (2, OLEV, NY_O, NX_O), jnp.float32, -0.24, 0.24) * block_scale(arg_keys[7], (2, OLEV, NY_O, NX_O), ((2, 8), (3, 4)), -0.4, 0.0), -0.24, 0.24),
        "exchange_coef": jnp.clip(jnp.exp(math.log(5.0) - 3.218876 * jax.random.uniform(arg_keys[8], (NY_O, NX_O), jnp.float32) ** block_scale(arg_keys[8], (NY_O, NX_O), ((0, 8), (1, 4)), -0.2, 0.2)), 0.2, 5.0),
        "surface_kind": set_ends(jax.random.randint(arg_keys[9], (NY_O, NX_O), 0, 3), jax.random.fold_in(arg_keys[9], 1), 0, 2).astype(jnp.int32),
        "ice_surface": gaussian(arg_keys[10], (NV, NY_O, NX_O), 1.0, 6.0, ((1, 8), (2, 4)), jnp.float32),
    }


def down_sweep(profile, diffusion):
    lev_count = profile.shape[1]
    coef_c = []
    coef_g = []
    recip_now = None
    for height in range(lev_count):
        denominator = jnp.ones_like(diffusion[0])
        right_side = profile[:, height]
        if height > 0:
            denominator = denominator + diffusion[height - 1] + diffusion[height - 1] * coef_c[-1]
            right_side = right_side + diffusion[height - 1] * coef_g[-1]
        if height < lev_count - 1:
            denominator = denominator + diffusion[height]
        recip_now = 1.0 / denominator
        coef_g.append(right_side * recip_now)
        if height < lev_count - 1:
            coef_c.append(-diffusion[height] * recip_now)
    return coef_c, coef_g, recip_now


def up_sweep(coef_c, coef_g, recip_now, surface_flux):
    column = coef_g[-1] + recip_now * surface_flux
    result = [column]
    for height in range(len(coef_c) - 1, -1, -1):
        column = coef_g[height] - coef_c[height] * column
        result.append(column)
    return jnp.stack(result[::-1], axis=1)


def advect(tracer, speed_rows, speed_cols):
    inner_rows = tracer[..., :, 1:-1]
    along_rows = speed_rows[:, :, 1:-1]
    face_rows = 0.5 * (along_rows[:, :-1] + along_rows[:, 1:])
    flow_rows = jnp.maximum(face_rows, 0.0) * inner_rows[..., :-1, :] + jnp.minimum(face_rows, 0.0) * inner_rows[..., 1:, :]
    inner_cols = tracer[..., 1:-1, :]
    along_cols = speed_cols[:, 1:-1, :]
    face_cols = 0.5 * (along_cols[..., :-1] + along_cols[..., 1:])
    flow_cols = jnp.maximum(face_cols, 0.0) * inner_cols[..., :-1] + jnp.minimum(face_cols, 0.0) * inner_cols[..., 1:]
    return tracer[..., 1:-1, 1:-1] - (flow_rows[..., 1:, :] - flow_rows[..., :-1, :]) - (flow_cols[..., 1:] - flow_cols[..., :-1])


def reference(atm_state, diffusivity, send_slot, atm_block, recv_row, remap_weight, ocean_tracer, ocean_velocity, exchange_coef, surface_kind, ice_surface):
    var_count = atm_state.shape[0]
    block_width = remap_weight.shape[1]
    devices = send_slot.shape[0]
    per_dev = send_slot.shape[1]
    fields = var_count + 1
    block_count = atm_state.shape[2] // devices // block_width
    coef_c, coef_g, recip_now = down_sweep(atm_state, diffusivity)
    packed = jnp.concatenate([coef_g[-1], recip_now[None]], axis=0).astype(jnp.bfloat16)
    by_device = packed.reshape(fields, devices, block_count, block_width).transpose(1, 2, 0, 3)
    weights = remap_weight.reshape(devices, per_dev, block_width, block_width)

    def forward(pieces):
        packed_dev, weight_dev, block_dev = pieces
        picked = jnp.take(packed_dev, block_dev, axis=0).astype(jnp.float32)
        return jnp.einsum('boa,bfa->bfo', weight_dev.astype(jnp.float32), picked)

    contrib = lax.map(forward, (by_device, weights, atm_block))
    owners = send_slot // CAP
    sources = jnp.arange(devices, dtype=jnp.int32)[:, None]
    rows_in = recv_row[owners, sources * CAP + send_slot % CAP]
    target = ((owners // N_OCN) * ORY + rows_in) * N_OCN + owners % N_OCN
    ocean_rows = ocean_tracer.shape[2]
    summed = jax.ops.segment_sum(contrib.reshape(-1, fields, block_width), target.reshape(-1), num_segments=ocean_rows * N_OCN)
    summed = summed.reshape(ocean_rows, N_OCN, fields, block_width).transpose(2, 0, 1, 3).reshape(fields, ocean_rows, -1)
    surface = jnp.where(surface_kind == 2, ice_surface, ocean_tracer[:, 0])
    coupling = jnp.where(surface_kind == 0, 0.0, exchange_coef)
    fluxes = coupling * (surface - summed[:var_count]) / (1.0 + coupling * summed[var_count])
    rounded = fluxes.astype(jnp.bfloat16)
    flux_rows = rounded.reshape(var_count, ocean_rows, N_OCN, block_width).transpose(1, 2, 0, 3).reshape(-1, var_count, block_width)

    def backward(pieces):
        weight_dev, target_dev, block_dev = pieces
        picked = jnp.take(flux_rows, target_dev, axis=0).astype(jnp.float32)
        spread = jnp.einsum('boa,bvo->bva', weight_dev.astype(jnp.float32), picked)
        return jax.ops.segment_sum(spread, block_dev, num_segments=block_count)

    returned = lax.map(backward, (weights, target, atm_block))
    surface_flux = returned.transpose(2, 0, 1, 3).reshape(var_count, -1)
    atm_new = up_sweep(coef_c, coef_g, recip_now, surface_flux)
    tracer = ocean_tracer.at[:, 0].add(-fluxes)
    padded_speed = jnp.pad(ocean_velocity, ((0, 0), (0, 0), (1, 1), (1, 1)))
    for substep in range(NSUB):
        padded = jnp.pad(tracer, ((0, 0), (0, 0), (1, 1), (1, 1)))
        tracer = advect(padded, padded_speed[0], padded_speed[1])
    return atm_new, tracer
```

```python
import functools

import jax
import jax.numpy as jnp
from jax import lax
from jax.experimental import pallas as pl
from jax.experimental.pallas import tpu as pltpu
from jax.sharding import PartitionSpec as P

NSUB = 4
SUB = 8
LANES = 128
F32 = jnp.float32
BF16 = jnp.bfloat16
VMEM = pl.BlockSpec(memory_space=pltpu.VMEM)
SMEM = pl.BlockSpec(memory_space=pltpu.SMEM)
ANY = pl.BlockSpec(memory_space=pl.ANY)


def shape(dims, kind=F32):
    return jax.ShapeDtypeStruct(dims, kind)


def round_up(value, unit):
    return -(-value // unit) * unit


def params(mib):
    return pltpu.CompilerParams(vmem_limit_bytes=mib * 2**20)


def cost(flops, moved):
    return pl.CostEstimate(flops=int(flops), bytes_accessed=int(moved), transcendentals=0)


def row_pack_kernel(tracer, speed, first, last, head, tail, sem):
    tracer_count, rows, _ = tracer.shape
    speed_count = speed.shape[0]
    total = tracer_count + speed_count
    copies = []
    for place, (start, into) in enumerate(((0, head), (rows - SUB, tail))):
        copies.append(
            pltpu.make_async_copy(
                tracer.at[:, pl.ds(start, SUB), :], into.at[pl.ds(0, tracer_count)], sem.at[place, 0]
            )
        )
        copies.append(
            pltpu.make_async_copy(
                speed.at[:, pl.ds(start, SUB), :],
                into.at[pl.ds(tracer_count, speed_count)],
                sem.at[place, 1],
            )
        )
    for copy in copies:
        copy.start()
    spare = head.shape[0] - total
    for into in (head, tail):
        into[pl.ds(total, spare)] = jnp.zeros((spare, SUB, LANES), F32)
    for copy in copies:
        copy.wait()
    for into, out, shift in ((head, first, 0), (tail, last, SUB - NSUB)):
        flat = into.reshape(into.shape[0] * SUB, LANES)
        for row in range(NSUB):
            for part in range(0, into.shape[0], 16):
                out[row, pl.ds(part, 16), :] = flat[
                    pl.ds(part * SUB + shift + row, 16, stride=SUB), :
                ].astype(BF16)


def row_pack(tracer, speed):
    total = round_up(tracer.shape[0] + speed.shape[0], 16)
    return pl.pallas_call(
        row_pack_kernel,
        out_shape=(shape((NSUB, total, LANES), BF16),) * 2,
        in_specs=[ANY, ANY],
        out_specs=(VMEM, VMEM),
        scratch_shapes=[
            pltpu.VMEM((total, SUB, LANES), F32),
            pltpu.VMEM((total, SUB, LANES), F32),
            pltpu.SemaphoreType.DMA((2, 2)),
        ],
        compiler_params=params(24),
        cost_estimate=cost(1e6, 4e6),
        name="row_pack",
    )(tracer, speed)


def down_kernel(
    profile, diffusion, slots, blocks, weight, coef_c, coef_g, recip, out, prof, diff, placed, total, held, sem
):
    fields, levels, columns = profile.shape
    count = columns // LANES
    width = fields + 1
    block_total = weight.shape[0]
    owners = out.shape[0]
    cap = out.shape[1] // width
    fetch = pltpu.make_async_copy(weight, held, sem)
    fetch.start()
    for field in range(fields):
        for low in range(0, levels, SUB):
            deep = min(SUB, levels - low)
            for block in range(count):
                prof[field, pl.ds(low * count + block, deep, stride=count), :] = profile[
                    field, pl.ds(low, deep), pl.ds(block * LANES, LANES)
                ]
    for low in range(0, levels - 1, SUB):
        deep = min(SUB, levels - 1 - low)
        for block in range(count):
            diff[pl.ds(low * count + block, deep, stride=count), :] = diffusion[
                pl.ds(low, deep), pl.ds(block * LANES, LANES)
            ]
    placed[...] = jnp.zeros(placed.shape, F32)
    total[...] = jnp.zeros(total.shape, F32)
    below = None
    for level in range(levels):
        here = pl.ds(level * count, count)
        rhs = [prof[field, here, :] for field in range(fields)]
        bottom = jnp.full((count, LANES), 1.0, F32)
        if level < levels - 1:
            above = diff[here, :]
            bottom = bottom + above
        if level > 0:
            bottom = bottom + below * (1.0 + c_now)
            rhs = [rhs[field] + below * g_now[field] for field in range(fields)]
        inverse = 1.0 / bottom
        g_now = [value * inverse for value in rhs]
        for field in range(fields):
            coef_g[field, here, :] = g_now[field]
        if level < levels - 1:
            c_now = -above * inverse
            coef_c[here, :] = c_now
            below = above
    recip[...] = inverse
    rows = cap * width
    for slot in range(cap):
        for field, value in enumerate(g_now + [inverse]):
            placed[slot, pl.ds(slot * width + field, count, stride=rows), :] = value
    fetch.wait()
    step = 8

    def body(group, _):
        results = []
        for inner in range(step):
            block = group * step + inner
            slot = slots[0, block]
            start = pl.multiple_of(blocks[0, block] * rows, rows)
            left = placed[slot % cap, pl.ds(start, rows), :].astype(BF16)
            results.append(
                lax.dot_general(
                    left, held[block], (((1,), (1,)), ((), ())), preferred_element_type=F32
                )
            )
        for inner in range(step):
            owner = slots[0, group * step + inner] // cap
            total[owner] = total[owner] + results[inner]
        return 0

    lax.fori_loop(0, block_total // step, body, 0)
    for owner in range(owners):
        out[owner] = total[owner].astype(BF16)


def down(profile, diffusion, slots, blocks, weight, owners, cap):
    fields, levels, columns = profile.shape
    count = columns // LANES
    rows = cap * (fields + 1)
    return pl.pallas_call(
        down_kernel,
        out_shape=(
            shape(((levels - 1) * count, LANES)),
            shape((fields, levels * count, LANES)),
            shape((count, LANES)),
            shape((owners, rows, LANES), BF16),
        ),
        in_specs=[VMEM, VMEM, SMEM, SMEM, ANY],
        out_specs=(VMEM, VMEM, VMEM, VMEM),
        scratch_shapes=[
            pltpu.VMEM((fields, levels * count, LANES), F32),
            pltpu.VMEM(((levels - 1) * count, LANES), F32),
            pltpu.VMEM((cap, count * rows, LANES), F32),
            pltpu.VMEM((owners, rows, LANES), F32),
            pltpu.VMEM(weight.shape, BF16),
            pltpu.SemaphoreType.DMA,
        ],
        compiler_params=params(40),
        cost_estimate=cost(1e7, 6e6),
        name="down_sweep",
    )(profile, diffusion, slots, blocks, weight)


def flux_kernel(arrived, recv, coef, kind, ice, surface, fluxes, answer, *, atm, ocn):
    fields, rows, _ = ice.shape
    width = fields + 1
    slot_total = recv.shape[1]
    chunk = answer.shape[1]
    back = arrived.shape[0] // answer.shape[0]
    spread = (
        lax.broadcasted_iota(jnp.int32, (slot_total, slot_total * width), 1) // width
        == lax.broadcasted_iota(jnp.int32, (slot_total, slot_total * width), 0)
    ).astype(F32).astype(BF16)
    row_of = jnp.broadcast_to(recv[...], (SUB, slot_total)).astype(F32).astype(BF16)
    row_of = jnp.dot(row_of, spread, preferred_element_type=F32)[0:1]
    lane = lax.broadcasted_iota(jnp.int32, (1, slot_total * width), 1)
    key = row_of.astype(jnp.int32) * width + lane % width
    line = lax.broadcasted_iota(jnp.int32, (width * rows, 1), 0)
    chosen = ((line % rows) * width + line // rows == key).astype(F32)
    summed = jnp.dot(chosen.astype(BF16), arrived[...], preferred_element_type=F32)
    hold = jnp.where(kind[...] != 0, coef[...], 0.0)
    over = 1.0 + hold * summed[fields * rows : (fields + 1) * rows]
    rounded = []
    for field in range(fields):
        top = jnp.where(kind[...] == 2, ice[field], surface[field, 0])
        value = hold * (top - summed[field * rows : (field + 1) * rows]) / over
        fluxes[field] = value
        rounded.append(value.astype(BF16).astype(F32))
    stacked = jnp.concatenate(rounded + [jnp.zeros((rows, LANES), F32)], axis=0).astype(BF16)
    turned = chosen.T.astype(BF16)
    returned = jnp.dot(turned, stacked, preferred_element_type=F32)
    answer[:, pl.ds(0, back), :] = returned.astype(BF16).reshape(answer.shape[0], back, LANES)
    answer[:, pl.ds(back, chunk - back), :] = jnp.zeros((answer.shape[0], chunk - back, LANES), BF16)

    source = lax.broadcasted_iota(jnp.int32, (LANES, 3 * LANES), 0)
    target = lax.broadcasted_iota(jnp.int32, (LANES, 3 * LANES), 1)
    own = source + NSUB
    south = source + rows + NSUB
    north = source - (rows - NSUB)
    pos = jnp.where(target < LANES, own, jnp.where(target < 2 * LANES, south, north))
    fits = (
        ((target < LANES) & (source < rows))
        | ((target >= LANES) & (target < 2 * LANES) & (source < NSUB))
        | ((target >= 2 * LANES) & (source >= rows - NSUB) & (source < rows))
    )
    place = (fits & ((pos % SUB) * SUB + pos // SUB == target % LANES)).astype(F32).astype(BF16)
    sides = []
    for field in range(fields):
        tall = jnp.concatenate([rounded[field], jnp.zeros((LANES - rows, LANES), F32)], axis=0)
        sides.append(jnp.dot(tall.T.astype(BF16), place, preferred_element_type=F32))
    blank = jnp.zeros((chunk - back - fields * NSUB, LANES), F32)
    i = lax.axis_index("atm")
    j = lax.axis_index("ocn")
    for di in (-1, 0, 1):
        for dj in (-1, 0, 1):
            if di == 0 and dj == 0:
                continue
            pieces = []
            for field in range(fields):
                if dj == 0:
                    low = 0 if di < 0 else rows - NSUB
                    pieces.append(rounded[field][low : low + NSUB])
                else:
                    low = 0 if dj < 0 else LANES - NSUB
                    part = {0: 0, -1: 1, 1: 2}[di] * LANES
                    pieces.append(sides[field][low : low + NSUB, part : part + LANES])
            tile = jnp.concatenate(pieces + [blank], axis=0).astype(BF16)

            @pl.when((i + di >= 0) & (i + di < atm) & (j + dj >= 0) & (j + dj < ocn))
            def _():
                answer[(i + di) * ocn + j + dj, pl.ds(back, chunk - back), :] = tile


def flux_step(arrived, recv, coef, kind, ice, tracer, owners, atm, ocn):
    fields, rows, _ = ice.shape
    back = arrived.shape[0] // owners
    chunk = back + round_up(fields * NSUB, 16)
    whole = lambda dims: pl.BlockSpec(dims, lambda g: (0,) * len(dims))
    return pl.pallas_call(
        functools.partial(flux_kernel, atm=atm, ocn=ocn),
        grid=(1,),
        out_shape=(shape(ice.shape), shape((owners, chunk, LANES), BF16)),
        in_specs=[
            whole(arrived.shape),
            whole(recv.shape),
            whole(coef.shape),
            whole(kind.shape),
            whole(ice.shape),
            whole((fields, 1, rows, LANES)),
        ],
        out_specs=(whole(ice.shape), whole((owners, chunk, LANES))),
        compiler_params=params(32),
        cost_estimate=cost(1e7, 1e6),
        name="flux_step",
    )(arrived, recv, coef, kind, ice, tracer)


def relayout_kernel(tracer, speed, north, south, out, west, east, raw, tall, done, fetched, stored):
    tracer_count, rows, _ = tracer.shape
    total = tracer_count + speed.shape[0]
    groups = out.shape[0]
    size = total // groups
    high = rows + 2 * NSUB

    def fetch(group):
        here = raw.at[pl.ds(group * size, size)]
        return here, fetched.at[group]

    for group in range(groups):
        into, sem = fetch(group)
        if (group + 1) * size <= tracer_count:
            source = tracer.at[pl.ds(group * size, size)]
        else:
            source = speed.at[pl.ds(group * size - tracer_count, size)]
        pltpu.make_async_copy(source, into, sem).start()
    padded_total = north.shape[1]
    tall[pl.ds(total * high, (padded_total - total) * high), :] = jnp.zeros(
        ((padded_total - total) * high, LANES), F32
    )
    for row in range(NSUB):
        for part in range(0, padded_total, 16):
            for halo, start in ((north, 0), (south, rows + NSUB)):
                tall[pl.ds(part * high + start + row, 16, stride=high), :] = halo[
                    row, pl.ds(part, 16), :
                ].astype(F32)

    def body(group, _):
        into, sem = fetch(group)
        pltpu.make_async_copy(into, into, sem).wait()
        for level in range(size):
            tall[pl.ds(pl.multiple_of(group * size * high, SUB) + level * high + NSUB, rows), :] = raw[
                group * size + level
            ]
        for fine in range(SUB):
            stack = tall[pl.ds(group * size * high + fine, LANES, stride=SUB), :]
            done[group, fine] = stack.T
        pltpu.make_async_copy(done.at[group], out.at[group], stored.at[group]).start()
        return 0

    lax.fori_loop(0, groups, body, 0)
    slabs = groups * SUB
    flat = done.reshape(slabs * LANES, LANES)
    for message, start in ((west, 0), (east, LANES - NSUB)):
        for column in range(NSUB):
            for part in range(0, message.shape[1], 16):
                pieces = []
                for low in (part, part + SUB):
                    if low < slabs:
                        pieces.append(flat[pl.ds(low * LANES + start + column, SUB, stride=LANES), :])
                    else:
                        pieces.append(jnp.zeros((SUB, LANES), F32))
                message[column, pl.ds(part, 16), :] = jnp.concatenate(pieces, axis=0).astype(BF16)
    for group in range(groups):
        pltpu.make_async_copy(done.at[group], out.at[group], stored.at[group]).wait()


def relayout(tracer, speed, north, south, size):
    rows = tracer.shape[1]
    total = tracer.shape[0] + speed.shape[0]
    groups = total // size
    slabs = round_up(groups * SUB, 16)
    return pl.pallas_call(
        relayout_kernel,
        out_shape=(
            shape((groups, SUB, LANES, LANES)),
            shape((NSUB, slabs, LANES), BF16),
            shape((NSUB, slabs, LANES), BF16),
        ),
        in_specs=[ANY, ANY, VMEM, VMEM],
        out_specs=(ANY, VMEM, VMEM),
        scratch_shapes=[
            pltpu.VMEM((total, rows, LANES), F32),
            pltpu.VMEM((north.shape[1] * (rows + 2 * NSUB), LANES), F32),
            pltpu.VMEM((groups, SUB, LANES, LANES), F32),
            pltpu.SemaphoreType.DMA((groups,)),
            pltpu.SemaphoreType.DMA((groups,)),
        ],
        compiler_params=params(48),
        cost_estimate=cost(1e7, 1.4e7),
        name="relayout",
    )(tracer, speed, north, south)


def up_kernel(answered, slots, blocks, weight, coef_c, coef_g, recip, out, held, sums, solved, sem):
    fields, levels, columns = out.shape
    count = columns // LANES
    width = fields + 1
    rows = sums.shape[1]
    cap = rows // width
    fetch = pltpu.make_async_copy(weight, held, sem)
    fetch.start()
    sums[...] = jnp.zeros(sums.shape, F32)
    slot_row = lax.broadcasted_iota(jnp.int32, (rows, LANES), 0) // width
    fetch.wait()
    step = 8

    def body(group, _):
        results = []
        for inner in range(step):
            block = group * step + inner
            left = answered[slots[0, block] // cap, pl.ds(0, rows), :]
            results.append(jnp.dot(left, held[block], preferred_element_type=F32))
        for inner in range(step):
            block = group * step + inner
            kept = jnp.where(slot_row == slots[0, block] % cap, results[inner], 0.0)
            sums[blocks[0, block]] = sums[blocks[0, block]] + kept
        return 0

    lax.fori_loop(0, weight.shape[0] // step, body, 0)
    flat = sums.reshape(count * rows, LANES)
    now = []
    last = pl.ds((levels - 1) * count, count)
    for field in range(fields):
        flux = flat[pl.ds(field, count, stride=rows), :]
        for slot in range(1, cap):
            flux = flux + flat[pl.ds(slot * width + field, count, stride=rows), :]
        now.append(coef_g[field, last, :] + recip[...] * flux)
        solved[field, last, :] = now[field]
    for level in range(levels - 2, -1, -1):
        here = pl.ds(level * count, count)
        for field in range(fields):
            now[field] = coef_g[field, here, :] - coef_c[here, :] * now[field]
            solved[field, here, :] = now[field]
    for field in range(fields):
        for low in range(0, levels, SUB):
            deep = min(SUB, levels - low)
            for block in range(count):
                out[field, pl.ds(low, deep), pl.ds(block * LANES, LANES)] = solved[
                    field, pl.ds(low * count + block, deep, stride=count), :
                ]


def up(answered, slots, blocks, weight, coef_c, coef_g, recip, levels, cap):
    fields = coef_g.shape[0]
    count = recip.shape[0]
    rows = cap * (fields + 1)
    return pl.pallas_call(
        up_kernel,
        out_shape=shape((fields, levels, count * LANES)),
        in_specs=[VMEM, SMEM, SMEM, ANY, VMEM, VMEM, VMEM],
        out_specs=VMEM,
        scratch_shapes=[
            pltpu.VMEM(weight.shape, BF16),
            pltpu.VMEM((count, rows, LANES), F32),
            pltpu.VMEM((fields, levels * count, LANES), F32),
            pltpu.SemaphoreType.DMA,
        ],
        compiler_params=params(40),
        cost_estimate=cost(1e7, 6e6),
        name="up_sweep",
    )(answered, slots, blocks, weight, coef_c, coef_g, recip)


def advect_kernel(
    laid, from_west, from_east, fluxes, answered, out, here, there, speed, coef, thin, halo, high, raw, fetched, stored,
    *, fields, atm, ocn
):
    groups = laid.shape[0]
    per = groups // (fields + 2)
    size = out.shape[0] // (fields * per)
    rows = out.shape[1]
    tall = rows + 2 * NSUB
    wide = here.shape[2]
    tiles = wide // SUB
    back = answered.shape[1] - round_up(fields * NSUB, 16)

    def fetch(group):
        if group < fields * per:
            into = here.at[group, :, pl.ds(SUB, LANES), :]
        else:
            into = speed.at[group - fields * per, :, pl.ds(SUB, LANES), :]
        return pltpu.make_async_copy(laid.at[group], into, fetched.at[group])

    for group in range(groups):
        fetch(group).start()
    for ref in (here, speed):
        ref[:, :, pl.ds(0, SUB), :] = jnp.zeros(ref.shape[:2] + (SUB, LANES), F32)
        ref[:, :, pl.ds(wide - SUB, SUB), :] = jnp.zeros(ref.shape[:2] + (SUB, LANES), F32)
    for side, message, start in ((0, from_west, SUB - NSUB), (1, from_east, wide - SUB)):
        for column in range(NSUB):
            halo[...] = message[column].astype(F32)
            for group in range(groups):
                ref, at = (here, group) if group < fields * per else (speed, group - fields * per)
                flat = ref.reshape(ref.shape[0] * SUB * wide, LANES)
                flat[pl.ds(at * SUB * wide + start + column, SUB, stride=wide), :] = halo[
                    pl.ds(group * SUB, SUB), :
                ]
    i = lax.axis_index("atm")
    j = lax.axis_index("ocn")

    def neighbour(di, dj):
        inside = (i + di >= 0) & (i + di < atm) & (j + dj >= 0) & (j + dj < ocn)
        index = jnp.where(inside, (i + di) * ocn + j + dj, 0)
        value = answered[index, pl.ds(back, answered.shape[1] - back), :].astype(F32)
        return jnp.where(inside, value, 0.0)

    up_rows = neighbour(-1, 0)
    down_rows = neighbour(1, 0)
    thin[...] = jnp.zeros(thin.shape, F32)
    for field in range(fields):
        thin[field, pl.ds(0, NSUB), :] = up_rows[field * NSUB : (field + 1) * NSUB]
        thin[field, pl.ds(NSUB, rows), :] = fluxes[field]
        thin[field, pl.ds(NSUB + rows, NSUB), :] = down_rows[field * NSUB : (field + 1) * NSUB]
    for field in range(fields):
        fetch(field * per).wait()
        for fine in range(SUB):
            few = thin[field, pl.ds(fine, SUB, stride=SUB), :]
            stack = jnp.concatenate([few, jnp.zeros((LANES - SUB, LANES), F32)], axis=0)
            at = (field * per, fine, pl.ds(SUB, LANES))
            here[at] = here[at] - stack.T
    lane = lax.broadcasted_iota(jnp.int32, (16, LANES), 1)
    for dj, start in ((-1, SUB - NSUB), (1, wide - SUB)):
        side = neighbour(-1, dj) + neighbour(0, dj) + neighbour(1, dj)
        for fine in range(SUB):
            moved = side if fine == 0 else pltpu.roll(side, LANES - SUB * fine, 1)
            moved = jnp.where(lane < SUB, moved, 0.0)
            for field in range(fields):
                at = (field * per, fine, pl.ds(start, NSUB))
                here[at] = here[at] - moved[field * NSUB : (field + 1) * NSUB]

    def shifted(ref, lead, tile, base, value, side):
        if side < 0:
            if isinstance(tile, int) and tile == 0:
                return pltpu.roll(value, 1, 0)
            return ref[lead + (pl.ds(base - 1, SUB),)]
        if isinstance(tile, int) and tile == tiles - 1:
            return pltpu.roll(value, SUB - 1, 0)
        return ref[lead + (pl.ds(base + 1, SUB),)]

    def coefs(group, tile):
        base = tile * SUB if isinstance(tile, int) else pl.multiple_of(tile * SUB, SUB)
        at = pl.ds(base, SUB)
        along = [speed[group, fine, at, :] for fine in range(SUB)]
        along.append(pltpu.roll(along[0], LANES - 1, 1))
        faces = [0.5 * (along[fine] + along[fine + 1]) for fine in range(SUB)]
        gain = [jnp.maximum(face, 0.0) for face in faces]
        lose = [gain[fine] - faces[fine] for fine in range(SUB)]
        gain_low = [pltpu.roll(gain[-1], 1, 1)] + gain[:-1]
        lose_low = [pltpu.roll(lose[-1], 1, 1)] + lose[:-1]
        for fine in range(SUB):
            lead = (per + group, fine)
            value = speed[lead + (at,)]
            above = 0.5 * (value + shifted(speed, lead, tile, base, value, 1))
            under = 0.5 * (value + shifted(speed, lead, tile, base, value, -1))
            gain_above = jnp.maximum(above, 0.0)
            gain_under = jnp.maximum(under, 0.0)
            lose_under = gain_under - under
            coef[0, fine, at, :] = 1.0 - (gain[fine] + lose_low[fine] + gain_above + lose_under)
            coef[1, fine, at, :] = gain_low[fine]
            coef[2, fine, at, :] = lose[fine]
            coef[3, fine, at, :] = gain_under
            coef[4, fine, at, :] = gain_above - above

    def update(group, src, dst, tile):
        base = tile * SUB if isinstance(tile, int) else pl.multiple_of(tile * SUB, SUB)
        at = pl.ds(base, SUB)
        lead = [src[0](field, group) for field in range(fields)]
        goal = [dst[0](field, group) for field in range(fields)]
        values = [[src[1][lead[f], fine, at, :] for fine in range(SUB)] for f in range(fields)]
        for fine in range(SUB):
            own, low, high_c, left, right = [coef[part, fine, at, :] for part in range(5)]
            for field in range(fields):
                value = values[field][fine]
                prior = values[field][fine - 1] if fine > 0 else pltpu.roll(values[field][-1], 1, 1)
                after = (
                    values[field][fine + 1]
                    if fine < SUB - 1
                    else pltpu.roll(values[field][0], LANES - 1, 1)
                )
                index = (lead[field], fine)
                before = shifted(src[1], index, tile, base, value, -1)
                behind = shifted(src[1], index, tile, base, value, 1)
                dst[1][goal[field], fine, at, :] = (
                    own * value + low * prior + high_c * after + left * before + right * behind
                )

    def sweep(work, edges):
        if edges:
            work(0)
            work(tiles - 1)
        lax.fori_loop(1, tiles - 1, lambda tile, _: (work(tile), 0)[1], 0, unroll=4)

    def body(group, _):
        for field in range(fields):
            at = field * per + group

            @pl.when(group > 0)
            def _():
                pltpu.make_async_copy(
                    laid.at[at], here.at[at, :, pl.ds(SUB, LANES), :], fetched.at[at]
                ).wait()

        for part in range(2):
            at = part * per + group
            pltpu.make_async_copy(
                laid.at[fields * per + at],
                speed.at[at, :, pl.ds(SUB, LANES), :],
                fetched.at[fields * per + at],
            ).wait()
        sweep(functools.partial(coefs, group), True)
        first = (lambda field, group: field * per + group, here)
        second = (lambda field, group: field, there)
        for substep in range(NSUB):
            src, dst = (first, second) if substep % 2 == 0 else (second, first)
            sweep(functools.partial(update, group, src, dst), substep < NSUB - 1)
        for field in range(fields):
            lead = field * per + group
            for fine in range(SUB):
                turned = here[lead, fine, pl.ds(SUB, LANES), :].T
                high[pl.ds(fine, LANES, stride=SUB), :] = turned
            base = lead * size
            for level in range(size):
                raw[base + level] = high[pl.ds(level * tall + NSUB, rows), :]
            pltpu.make_async_copy(
                raw.at[pl.ds(base, size)], out.at[pl.ds(base, size)], stored.at[lead]
            ).start()
        return 0

    lax.fori_loop(0, per, body, 0)
    for lead in range(fields * per):
        pltpu.make_async_copy(
            raw.at[pl.ds(lead * size, size)], out.at[pl.ds(lead * size, size)], stored.at[lead]
        ).wait()


def advect(laid, from_west, from_east, fluxes, answered, rows, size, atm, ocn):
    fields = fluxes.shape[0]
    groups = laid.shape[0]
    per = groups // (fields + 2)
    wide = LANES + 2 * SUB
    total = fields * per * size
    return pl.pallas_call(
        functools.partial(advect_kernel, fields=fields, atm=atm, ocn=ocn),
        out_shape=shape((total, rows, LANES)),
        in_specs=[ANY, VMEM, VMEM, VMEM, VMEM],
        out_specs=ANY,
        scratch_shapes=[
            pltpu.VMEM((fields * per, SUB, wide, LANES), F32),
            pltpu.VMEM((fields, SUB, wide, LANES), F32),
            pltpu.VMEM((2 * per, SUB, wide, LANES), F32),
            pltpu.VMEM((5, SUB, wide, LANES), F32),
            pltpu.VMEM((fields, SUB * SUB, LANES), F32),
            pltpu.VMEM((from_west.shape[1], LANES), F32),
            pltpu.VMEM((SUB * LANES, LANES), F32),
            pltpu.VMEM((total, rows, LANES), F32),
            pltpu.SemaphoreType.DMA((groups,)),
            pltpu.SemaphoreType.DMA((fields * per,)),
        ],
        compiler_params=params(48),
        cost_estimate=cost(5e7, 1.2e7),
        name="advect",
    )(laid, from_west, from_east, fluxes, answered)


def per_device(
    atm_state,
    diffusivity,
    send_slot,
    atm_block,
    recv_row,
    remap_weight,
    ocean_tracer,
    ocean_velocity,
    exchange_coef,
    surface_kind,
    ice_surface,
):
    atm, ocn = lax.axis_size("atm"), lax.axis_size("ocn")
    owners = atm * ocn
    fields, levels, _ = atm_state.shape
    cap = recv_row.shape[1] // owners
    depth, rows, columns = ocean_tracer.shape[1:]
    most = LANES // ((rows + 2 * NSUB) // SUB)
    size = max(count for count in range(1, most + 1) if depth % count == 0)
    tracer = ocean_tracer.reshape(-1, rows, columns)
    speed = ocean_velocity.reshape(-1, rows, columns)

    def neighbours(axis):
        count = lax.axis_size(axis)
        up = [(place, place + 1) for place in range(count - 1)]
        return up, [(target, source) for source, target in up]

    forward, backward = neighbours("atm")
    first, last = row_pack(tracer, speed)
    south = lax.ppermute(first, "atm", backward)
    north = lax.ppermute(last, "atm", forward)
    coef_c, coef_g, recip, outgoing = down(
        atm_state, diffusivity, send_slot, atm_block, remap_weight, owners, cap
    )
    arrived = lax.all_to_all(outgoing, ("atm", "ocn"), split_axis=0, concat_axis=0, tiled=True)
    fluxes, answer = flux_step(
        arrived.reshape(-1, LANES), recv_row, exchange_coef, surface_kind, ice_surface,
        ocean_tracer, owners, atm, ocn,
    )
    answered = lax.all_to_all(answer, ("atm", "ocn"), split_axis=0, concat_axis=0, tiled=True)
    laid, to_west, to_east = relayout(tracer, speed, north, south, size)
    forward, backward = neighbours("ocn")
    from_east = lax.ppermute(to_west, "ocn", backward)
    from_west = lax.ppermute(to_east, "ocn", forward)
    atm_new = up(
        answered, send_slot, atm_block, remap_weight, coef_c, coef_g, recip, levels, cap
    )
    ocean_new = advect(laid, from_west, from_east, fluxes, answered, rows, size, atm, ocn)
    return atm_new, ocean_new.reshape(ocean_tracer.shape)


def solution(mesh):
    placed = (
        P(None, None, ("atm", "ocn")),
        P(None, ("atm", "ocn")),
        P(("atm", "ocn"), None),
        P(("atm", "ocn"), None),
        P(("atm", "ocn"), None),
        P(("atm", "ocn"), None, None),
        P(None, None, "atm", "ocn"),
        P(None, None, "atm", "ocn"),
        P("atm", "ocn"),
        P("atm", "ocn"),
        P(None, "atm", "ocn"),
    )
    return jax.shard_map(
        per_device,
        mesh=mesh,
        in_specs=placed,
        out_specs=(P(None, None, ("atm", "ocn")), P(None, None, "atm", "ocn")),
        check_vma=False,
    )
```

```python
import functools

import jax
import jax.numpy as jnp
from jax import lax
from jax.experimental import pallas as pl
from jax.experimental.pallas import tpu as pltpu
from jax.sharding import PartitionSpec as P

NSUB = 4
SUB = 8
LANES = 128
GRANT = 52
F32 = jnp.float32
BF16 = jnp.bfloat16
VMEM = pl.BlockSpec(memory_space=pltpu.VMEM)
ANY = pl.BlockSpec(memory_space=pl.ANY)


def shape(dims, kind=F32):
    return jax.ShapeDtypeStruct(dims, kind)


def round_up(value, unit):
    return -(-value // unit) * unit


def params(mib):
    return pltpu.CompilerParams(vmem_limit_bytes=mib * 2**20)


def cost(flops, moved):
    return pl.CostEstimate(flops=int(flops), bytes_accessed=int(moved), transcendentals=0)


def row_pack_kernel(tracer, speed, first, last, head, tail, sem):
    tracer_count, rows, _ = tracer.shape
    speed_count = speed.shape[0]
    total = tracer_count + speed_count
    copies = []
    for place, (start, into) in enumerate(((0, head), (rows - SUB, tail))):
        copies.append(
            pltpu.make_async_copy(
                tracer.at[:, pl.ds(start, SUB), :], into.at[pl.ds(0, tracer_count)], sem.at[place, 0]
            )
        )
        copies.append(
            pltpu.make_async_copy(
                speed.at[:, pl.ds(start, SUB), :],
                into.at[pl.ds(tracer_count, speed_count)],
                sem.at[place, 1],
            )
        )
    for copy in copies:
        copy.start()
    spare = head.shape[0] - total
    for into in (head, tail):
        into[pl.ds(total, spare)] = jnp.zeros((spare, SUB, LANES), F32)
    for copy in copies:
        copy.wait()
    for into, out, shift in ((head, first, 0), (tail, last, SUB - NSUB)):
        flat = into.reshape(into.shape[0] * SUB, LANES)
        for row in range(NSUB):
            for part in range(0, into.shape[0], 16):
                out[row, pl.ds(part, 16), :] = flat[
                    pl.ds(part * SUB + shift + row, 16, stride=SUB), :
                ].astype(BF16)


def row_pack(tracer, speed):
    total = round_up(tracer.shape[0] + speed.shape[0], 16)
    return pl.pallas_call(
        row_pack_kernel,
        out_shape=(shape((NSUB, total, LANES), BF16),) * 2,
        in_specs=[ANY, ANY],
        out_specs=(VMEM, VMEM),
        scratch_shapes=[
            pltpu.VMEM((total, SUB, LANES), F32),
            pltpu.VMEM((total, SUB, LANES), F32),
            pltpu.SemaphoreType.DMA((2, 2)),
        ],
        compiler_params=params(GRANT),
        cost_estimate=cost(1e6, 4e6),
        name="row_pack",
    )(tracer, speed)


def down_kernel(
    profile, diffusion, slots, blocks, weight, after, coef_c, coef_g, recip, out,
    given, mixing, slot, block, held, prof, diff, made_c, made_g, made_r, placed, total, sent, sem, level_sem,
):
    fields, levels, columns = profile.shape
    count = columns // LANES
    width = fields + 1
    owners = out.shape[0]
    cap = out.shape[1] // width
    rows = cap * width
    lows = range(0, levels, SUB)

    def part(index):
        low = index * SUB
        deep = min(SUB, levels - low)
        return low, deep, min(SUB, levels - 1 - low)

    loads = []
    for index, low in enumerate(lows):
        low, deep, deep_k = part(index)
        pair = [
            pltpu.make_async_copy(
                diffusion.at[pl.ds(low, deep_k)], mixing.at[pl.ds(low, deep_k)], level_sem.at[index, 0]
            ),
            pltpu.make_async_copy(
                profile.at[:, pl.ds(low, deep), :], given.at[:, pl.ds(low, deep), :], level_sem.at[index, 1]
            ),
        ]
        for copy in pair:
            copy.start()
        loads.append(pair)
    others = [
        pltpu.make_async_copy(weight, held, sem.at[0]),
        pltpu.make_async_copy(slots, slot, sem.at[1]),
        pltpu.make_async_copy(blocks, block, sem.at[2]),
    ]
    for copy in others:
        copy.start()
    placed[...] = jnp.zeros(placed.shape, F32)
    total[...] = jnp.zeros(total.shape, F32)
    below = None
    for index, _ in enumerate(lows):
        low, deep, deep_k = part(index)
        for copy in loads[index]:
            copy.wait()
        for place in range(count):
            across = pl.ds(place * LANES, LANES)
            diff[pl.ds(low * count + place, deep_k, stride=count), :] = mixing[pl.ds(low, deep_k), across]
            for field in range(fields):
                prof[field, pl.ds(low * count + place, deep, stride=count), :] = given[
                    field, pl.ds(low, deep), across
                ]
        for level in range(low, low + deep):
            here = pl.ds(level * count, count)
            rhs = [prof[field, here, :] for field in range(fields)]
            bottom = jnp.full((count, LANES), 1.0, F32)
            if level < levels - 1:
                above = diff[here, :]
                bottom = bottom + above
            if level > 0:
                bottom = bottom + below * (1.0 + c_now)
                rhs = [rhs[field] + below * g_now[field] for field in range(fields)]
            inverse = 1.0 / bottom
            g_now = [value * inverse for value in rhs]
            for field in range(fields):
                made_g[field, here, :] = g_now[field]
            if level < levels - 1:
                c_now = -above * inverse
                made_c[here, :] = c_now
                below = above
    made_r[...] = inverse
    results_out = [
        pltpu.make_async_copy(made_c, coef_c, sem.at[3]),
        pltpu.make_async_copy(made_g, coef_g, sem.at[4]),
        pltpu.make_async_copy(made_r, recip, sem.at[5]),
    ]
    for copy in results_out:
        copy.start()
    for number in range(cap):
        for field, value in enumerate(g_now + [inverse]):
            placed[number, pl.ds(number * width + field, count, stride=rows), :] = value
    for copy in others:
        copy.wait()
    step = 8

    def body(group, _):
        results = []
        for inner in range(step):
            at = group * step + inner
            start = pl.multiple_of(block[0, at] * rows, rows)
            left = placed[slot[0, at] % cap, pl.ds(start, rows), :].astype(BF16)
            results.append(
                lax.dot_general(
                    left, held[at], (((1,), (1,)), ((), ())), preferred_element_type=F32
                )
            )
        for inner in range(step):
            owner = slot[0, group * step + inner] // cap
            total[owner] = total[owner] + results[inner]
        return 0

    lax.fori_loop(0, held.shape[0] // step, body, 0)
    for owner in range(owners):
        sent[owner] = total[owner].astype(BF16)
    final = pltpu.make_async_copy(sent, out, sem.at[6])
    final.start()
    for copy in results_out:
        copy.wait()
    final.wait()


def down(profile, diffusion, slots, blocks, weight, after, owners, cap):
    fields, levels, columns = profile.shape
    count = columns // LANES
    rows = cap * (fields + 1)
    padded = round_up(levels, SUB)
    return pl.pallas_call(
        down_kernel,
        out_shape=(
            shape(((levels - 1) * count, LANES)),
            shape((fields, levels * count, LANES)),
            shape((count, LANES)),
            shape((owners, rows, LANES), BF16),
        ),
        in_specs=[ANY] * 5 + [ANY],
        out_specs=(ANY,) * 4,
        scratch_shapes=[
            pltpu.VMEM((fields, padded, columns), F32),
            pltpu.VMEM((padded, columns), F32),
            pltpu.SMEM(slots.shape, jnp.int32),
            pltpu.SMEM(blocks.shape, jnp.int32),
            pltpu.VMEM(weight.shape, BF16),
            pltpu.VMEM((fields, levels * count, LANES), F32),
            pltpu.VMEM(((levels - 1) * count, LANES), F32),
            pltpu.VMEM(((levels - 1) * count, LANES), F32),
            pltpu.VMEM((fields, levels * count, LANES), F32),
            pltpu.VMEM((count, LANES), F32),
            pltpu.VMEM((cap, count * rows, LANES), F32),
            pltpu.VMEM((owners, rows, LANES), F32),
            pltpu.VMEM((owners, rows, LANES), BF16),
            pltpu.SemaphoreType.DMA((7,)),
            pltpu.SemaphoreType.DMA((padded // SUB, 2)),
        ],
        compiler_params=params(GRANT),
        cost_estimate=cost(1e7, 6e6),
        name="down_sweep",
    )(profile, diffusion, slots, blocks, weight, after)


def flux_kernel(
    arrived_at, recv_at, coef_at, kind_at, ice_at, tracer, after, later, fluxes_at, answer_at,
    arrived, recv, coef, kind, ice, surface, fluxes, answer, sem, *, atm, ocn
):
    loads = [
        pltpu.make_async_copy(source, into, sem.at[place])
        for place, (source, into) in enumerate(
            (
                (recv_at, recv),
                (arrived_at, arrived),
                (coef_at, coef),
                (kind_at, kind),
                (ice_at, ice),
                (tracer.at[:, pl.ds(0, 1)], surface),
            )
        )
    ]
    for copy in loads:
        copy.start()
    fields, rows, _ = ice.shape
    width = fields + 1
    slot_total = recv.shape[1]
    chunk = answer.shape[1]
    back = arrived.shape[0] // answer.shape[0]
    spread = (
        lax.broadcasted_iota(jnp.int32, (slot_total, slot_total * width), 1) // width
        == lax.broadcasted_iota(jnp.int32, (slot_total, slot_total * width), 0)
    ).astype(F32).astype(BF16)
    loads[0].wait()
    row_of = jnp.broadcast_to(recv[...], (SUB, slot_total)).astype(F32).astype(BF16)
    row_of = jnp.dot(row_of, spread, preferred_element_type=F32)[0:1]
    lane = lax.broadcasted_iota(jnp.int32, (1, slot_total * width), 1)
    key = row_of.astype(jnp.int32) * width + lane % width
    line = lax.broadcasted_iota(jnp.int32, (width * rows, 1), 0)
    chosen = ((line % rows) * width + line // rows == key).astype(F32)
    for copy in loads[1:]:
        copy.wait()
    summed = jnp.dot(chosen.astype(BF16), arrived[...], preferred_element_type=F32)
    hold = jnp.where(kind[...] != 0, coef[...], 0.0)
    over = 1.0 + hold * summed[fields * rows : (fields + 1) * rows]
    rounded = []
    for field in range(fields):
        top = jnp.where(kind[...] == 2, ice[field], surface[field, 0])
        value = hold * (top - summed[field * rows : (field + 1) * rows]) / over
        fluxes[field] = value
        rounded.append(value.astype(BF16).astype(F32))
    stacked = jnp.concatenate(rounded + [jnp.zeros((rows, LANES), F32)], axis=0).astype(BF16)
    turned = chosen.T.astype(BF16)
    returned = jnp.dot(turned, stacked, preferred_element_type=F32)
    answer[:, pl.ds(0, back), :] = returned.astype(BF16).reshape(answer.shape[0], back, LANES)
    answer[:, pl.ds(back, chunk - back), :] = jnp.zeros((answer.shape[0], chunk - back, LANES), BF16)

    source = lax.broadcasted_iota(jnp.int32, (LANES, 3 * LANES), 0)
    target = lax.broadcasted_iota(jnp.int32, (LANES, 3 * LANES), 1)
    own = source + NSUB
    south = source + rows + NSUB
    north = source - (rows - NSUB)
    pos = jnp.where(target < LANES, own, jnp.where(target < 2 * LANES, south, north))
    fits = (
        ((target < LANES) & (source < rows))
        | ((target >= LANES) & (target < 2 * LANES) & (source < NSUB))
        | ((target >= 2 * LANES) & (source >= rows - NSUB) & (source < rows))
    )
    place = (fits & ((pos % SUB) * SUB + pos // SUB == target % LANES)).astype(F32).astype(BF16)
    sides = []
    for field in range(fields):
        tall = jnp.concatenate([rounded[field], jnp.zeros((LANES - rows, LANES), F32)], axis=0)
        sides.append(jnp.dot(tall.T.astype(BF16), place, preferred_element_type=F32))
    blank = jnp.zeros((chunk - back - fields * NSUB, LANES), F32)
    i = lax.axis_index("atm")
    j = lax.axis_index("ocn")
    for di in (-1, 0, 1):
        for dj in (-1, 0, 1):
            if di == 0 and dj == 0:
                continue
            pieces = []
            for field in range(fields):
                if dj == 0:
                    low = 0 if di < 0 else rows - NSUB
                    pieces.append(rounded[field][low : low + NSUB])
                else:
                    low = 0 if dj < 0 else LANES - NSUB
                    part = {0: 0, -1: 1, 1: 2}[di] * LANES
                    pieces.append(sides[field][low : low + NSUB, part : part + LANES])
            tile = jnp.concatenate(pieces + [blank], axis=0).astype(BF16)

            @pl.when((i + di >= 0) & (i + di < atm) & (j + dj >= 0) & (j + dj < ocn))
            def _():
                answer[(i + di) * ocn + j + dj, pl.ds(back, chunk - back), :] = tile

    stores = [
        pltpu.make_async_copy(answer, answer_at, sem.at[6]),
        pltpu.make_async_copy(fluxes, fluxes_at, sem.at[7]),
    ]
    for copy in stores:
        copy.start()
    for copy in stores:
        copy.wait()


def flux_step(arrived, recv, coef, kind, ice, tracer, after, later, owners, atm, ocn):
    fields, rows, _ = ice.shape
    back = arrived.shape[0] // owners
    chunk = back + round_up(fields * NSUB, 16)
    return pl.pallas_call(
        functools.partial(flux_kernel, atm=atm, ocn=ocn),
        out_shape=(shape(ice.shape), shape((owners, chunk, LANES), BF16)),
        in_specs=[ANY] * 8,
        out_specs=(ANY, ANY),
        scratch_shapes=[
            pltpu.VMEM(arrived.shape, BF16),
            pltpu.VMEM(recv.shape, jnp.int32),
            pltpu.VMEM(coef.shape, F32),
            pltpu.VMEM(kind.shape, jnp.int32),
            pltpu.VMEM(ice.shape, F32),
            pltpu.VMEM((fields, 1, rows, LANES), F32),
            pltpu.VMEM(ice.shape, F32),
            pltpu.VMEM((owners, chunk, LANES), BF16),
            pltpu.SemaphoreType.DMA((8,)),
        ],
        compiler_params=params(GRANT),
        cost_estimate=cost(1e7, 1e6),
        name="flux_step",
    )(arrived, recv, coef, kind, ice, tracer, after, later)


def spot(column, across):
    return column % across * SUB + column // across


def relayout_kernel(
    tracer, speed, north_at, south_at, out, west, east, north, south, raw, tall, plain, done, sem, fetched, stored
):
    halos = [
        pltpu.make_async_copy(north_at, north, sem.at[0]),
        pltpu.make_async_copy(south_at, south, sem.at[1]),
    ]
    for copy in halos:
        copy.start()
    tracer_count, rows, _ = tracer.shape
    total = tracer_count + speed.shape[0]
    groups = out.shape[0]
    size = total // groups
    high = rows + 2 * NSUB
    wide = out.shape[2]
    across = wide // SUB

    def fetch(group):
        here = raw.at[pl.ds(group * size, size)]
        return here, fetched.at[group]

    for group in range(groups):
        into, sem = fetch(group)
        if (group + 1) * size <= tracer_count:
            source = tracer.at[pl.ds(group * size, size)]
        else:
            source = speed.at[pl.ds(group * size - tracer_count, size)]
        pltpu.make_async_copy(source, into, sem).start()
    padded_total = north.shape[1]
    tall[pl.ds(total * high, (padded_total - total) * high), :] = jnp.zeros(
        ((padded_total - total) * high, LANES), F32
    )
    for copy in halos:
        copy.wait()
    for row in range(NSUB):
        for part in range(0, padded_total, 16):
            for halo, start in ((north, 0), (south, rows + NSUB)):
                tall[pl.ds(part * high + start + row, 16, stride=high), :] = halo[
                    row, pl.ds(part, 16), :
                ].astype(F32)

    def body(group, _):
        into, sem = fetch(group)
        pltpu.make_async_copy(into, into, sem).wait()
        for level in range(size):
            tall[pl.ds(pl.multiple_of(group * size * high, SUB) + level * high + NSUB, rows), :] = raw[
                group * size + level
            ]
        for fine in range(SUB):
            stack = tall[pl.ds(group * size * high + fine, LANES, stride=SUB), :]
            plain[fine, pl.ds(SUB, LANES), :] = stack.T
            for step in range(across):
                done[group, fine, pl.ds(step * SUB, SUB), :] = plain[
                    fine, pl.ds(SUB - NSUB + step, SUB, stride=across), :
                ]
        pltpu.make_async_copy(done.at[group], out.at[group], stored.at[group]).start()
        return 0

    lax.fori_loop(0, groups, body, 0)
    slabs = groups * SUB
    flat = done.reshape(slabs * wide, LANES)
    for message, start in ((west, NSUB), (east, wide - 2 * NSUB)):
        for column in range(NSUB):
            at = spot(start + column, across)
            for part in range(0, message.shape[1], 16):
                pieces = []
                for low in (part, part + SUB):
                    if low < slabs:
                        pieces.append(flat[pl.ds(low * wide + at, SUB, stride=wide), :])
                    else:
                        pieces.append(jnp.zeros((SUB, LANES), F32))
                message[column, pl.ds(part, 16), :] = jnp.concatenate(pieces, axis=0).astype(BF16)
    for group in range(groups):
        pltpu.make_async_copy(done.at[group], out.at[group], stored.at[group]).wait()


def relayout(tracer, speed, north, south, size):
    rows = tracer.shape[1]
    total = tracer.shape[0] + speed.shape[0]
    groups = total // size
    slabs = round_up(groups * SUB, 16)
    wide = LANES + 2 * NSUB
    return pl.pallas_call(
        relayout_kernel,
        out_shape=(
            shape((groups, SUB, wide, LANES)),
            shape((NSUB, slabs, LANES), BF16),
            shape((NSUB, slabs, LANES), BF16),
        ),
        in_specs=[ANY, ANY, ANY, ANY],
        out_specs=(ANY, VMEM, VMEM),
        scratch_shapes=[
            pltpu.VMEM(north.shape, BF16),
            pltpu.VMEM(south.shape, BF16),
            pltpu.VMEM((total, rows, LANES), F32),
            pltpu.VMEM((north.shape[1] * (rows + 2 * NSUB), LANES), F32),
            pltpu.VMEM((SUB, LANES + 2 * SUB, LANES), F32),
            pltpu.VMEM((groups, SUB, wide, LANES), F32),
            pltpu.SemaphoreType.DMA((2,)),
            pltpu.SemaphoreType.DMA((groups,)),
            pltpu.SemaphoreType.DMA((groups,)),
        ],
        compiler_params=params(GRANT),
        cost_estimate=cost(1e7, 1.4e7),
        name="relayout",
    )(tracer, speed, north, south)


def up_part(
    answer, out, slot, block, held, made_c, made_g, made_r, sums, solved, final, first, weights, later, out_sem
):
    fields, levels, columns = out.shape
    count = columns // LANES
    width = fields + 1
    rows = sums.shape[1]
    cap = rows // width
    parts = len(weights)
    share = held.shape[0] // parts
    sums[...] = jnp.zeros(sums.shape, F32)
    slot_row = lax.broadcasted_iota(jnp.int32, (rows, LANES), 0) // width
    step = 8

    def body(group, _):
        results = []
        for inner in range(step):
            at = group * step + inner
            left = answer[slot[0, at] // cap, pl.ds(0, rows), :]
            results.append(jnp.dot(left, held[at], preferred_element_type=F32))
        for inner in range(step):
            at = group * step + inner
            kept = jnp.where(slot_row == slot[0, at] % cap, results[inner], 0.0)
            sums[block[0, at]] = sums[block[0, at]] + kept
        return 0

    for copy in first:
        copy.wait()
    for part in range(parts):
        weights[part].wait()
        lax.fori_loop(part * share // step, (part + 1) * share // step, body, 0)
    for copy in later:
        copy.wait()
    flat = sums.reshape(count * rows, LANES)
    now = []
    last = pl.ds((levels - 1) * count, count)
    for field in range(fields):
        flux = flat[pl.ds(field, count, stride=rows), :]
        for number in range(1, cap):
            flux = flux + flat[pl.ds(number * width + field, count, stride=rows), :]
        now.append(made_g[field, last, :] + made_r[...] * flux)
        solved[field, last, :] = now[field]
    copies = []
    for low in reversed(range(0, levels, SUB)):
        deep = min(SUB, levels - low)
        for level in range(min(low + deep, levels - 1) - 1, low - 1, -1):
            here = pl.ds(level * count, count)
            for field in range(fields):
                now[field] = made_g[field, here, :] - made_c[here, :] * now[field]
                solved[field, here, :] = now[field]
        for field in range(fields):
            for place in range(count):
                final[field, pl.ds(low, deep), pl.ds(place * LANES, LANES)] = solved[
                    field, pl.ds(low * count + place, deep, stride=count), :
                ]
        copies.append(
            pltpu.make_async_copy(
                final.at[:, pl.ds(low, deep), :], out.at[:, pl.ds(low, deep), :], out_sem.at[low // SUB]
            )
        )
        copies[-1].start()
    return copies


class Transport:
    def __init__(self, laid, from_west_at, from_east_at, out, scratch, fields, first, count):
        self.laid, self.out, self.fields, self.first, self.count = laid, out, fields, first, count
        (
            self.from_west, self.from_east, self.here, self.there, self.speed, self.along, self.cross,
            self.halo, self.plain, self.high, self.raw, self.sem, self.fetched, self.stored,
        ) = scratch
        self.per = laid.shape[0] // (fields + 2)
        self.size = out.shape[0] // (fields * self.per)
        self.rows = out.shape[1]
        self.wide = laid.shape[2]
        self.across = self.wide // SUB
        self.smalls = [
            pltpu.make_async_copy(from_west_at, self.from_west, self.sem.at[0]),
            pltpu.make_async_copy(from_east_at, self.from_east, self.sem.at[1]),
        ]

    @staticmethod
    def scratch(laid_shape, message_shape, out_rows, size, fields, count):
        groups, _, wide, _ = laid_shape
        return [
            pltpu.VMEM(message_shape, BF16),
            pltpu.VMEM(message_shape, BF16),
            pltpu.VMEM((fields * count, SUB, wide, LANES), F32),
            pltpu.VMEM((fields, SUB, wide, LANES), F32),
            pltpu.VMEM((2 * count, SUB, wide, LANES), F32),
            pltpu.VMEM((SUB + 1, wide, LANES), F32),
            pltpu.VMEM((SUB, wide, LANES), F32),
            pltpu.VMEM((2,) + message_shape, F32),
            pltpu.VMEM((SUB, LANES + 2 * SUB, LANES), F32),
            pltpu.VMEM((fields, SUB * LANES, LANES), F32),
            pltpu.VMEM((fields * count * size, out_rows, LANES), F32),
            pltpu.SemaphoreType.DMA((2,)),
            pltpu.SemaphoreType.DMA((fields + 2, count)),
            pltpu.SemaphoreType.DMA((fields, count)),
        ]

    def fetch(self, array, turn):
        group = array * self.per + self.first + turn
        if array < self.fields:
            into = self.here.at[array * self.count + turn]
        else:
            into = self.speed.at[(array - self.fields) * self.count + turn]
        return pltpu.make_async_copy(self.laid.at[group], into, self.fetched.at[array, turn])

    def store(self, field, turn):
        start = (field * self.per + self.first + turn) * self.size
        return pltpu.make_async_copy(
            self.raw.at[pl.ds((field * self.count + turn) * self.size, self.size)],
            self.out.at[pl.ds(start, self.size)],
            self.stored.at[field, turn],
        )

    def start(self, turn):
        for array in range(self.fields + 2):
            self.fetch(array, turn).start()
        if turn == 0:
            for copy in self.smalls:
                copy.start()

    def messages(self):
        for copy in self.smalls:
            copy.wait()
        for column in range(NSUB):
            self.halo[0, column] = self.from_west[column].astype(F32)
            self.halo[1, column] = self.from_east[column].astype(F32)

    def ready(self, turn):
        wide = self.wide
        for array in range(self.fields + 2):
            self.fetch(array, turn).wait()
            if array < self.fields:
                ref, at = self.here, array * self.count + turn
            else:
                ref, at = self.speed, (array - self.fields) * self.count + turn
            group = array * self.per + self.first + turn
            flat = ref.reshape(ref.shape[0] * SUB * wide, LANES)
            for side in range(2):
                for column in range(NSUB):
                    to = spot(column if side == 0 else wide - NSUB + column, self.across)
                    flat[pl.ds(at * (SUB * wide) + to, SUB, stride=wide), :] = self.halo[
                        side, column, pl.ds(group * SUB, SUB), :
                    ]

    def force(self, neighbour, fluxes, thin):
        fields, rows, across, plain = self.fields, self.rows, self.across, self.plain
        thin[...] = jnp.zeros(thin.shape, F32)
        up_rows = neighbour(-1, 0)
        down_rows = neighbour(1, 0)
        for field in range(fields):
            thin[field, pl.ds(0, NSUB), :] = up_rows[field * NSUB : (field + 1) * NSUB]
            thin[field, pl.ds(NSUB, rows), :] = fluxes[field]
            thin[field, pl.ds(NSUB + rows, NSUB), :] = down_rows[field * NSUB : (field + 1) * NSUB]
        lane = lax.broadcasted_iota(jnp.int32, (16, LANES), 1)
        sides = [sum(neighbour(di, dj) for di in (-1, 0, 1)) for dj in (-1, 1)]
        for fine in range(SUB):
            moved = []
            for side in sides:
                turned = side if fine == 0 else pltpu.roll(side, LANES - SUB * fine, 1)
                moved.append(jnp.where(lane < SUB, turned, 0.0))
            for field in range(fields):
                few = thin[field, pl.ds(fine, SUB, stride=SUB), :]
                stack = jnp.concatenate([few, jnp.zeros((LANES - SUB, LANES), F32)], axis=0)
                plain[field, pl.ds(SUB, LANES), :] = stack.T
                plain[field, pl.ds(SUB - NSUB, NSUB), :] = moved[0][field * NSUB : (field + 1) * NSUB]
                plain[field, pl.ds(SUB + LANES, NSUB), :] = moved[1][field * NSUB : (field + 1) * NSUB]
                for step in range(across):
                    at = (field * self.count, fine, pl.ds(step * SUB, SUB))
                    self.here[at] = (
                        self.here[at] - plain[field, pl.ds(SUB - NSUB + step, SUB, stride=across), :]
                    )

    def faces(self, turn):
        speed, along, cross, across = self.speed, self.along, self.cross, self.across
        for step in range(across):
            at = pl.ds(step * SUB, SUB)
            after = pl.ds(step * SUB + SUB, SUB) if step < across - 1 else pl.ds(1, SUB)
            rows_here = [speed[turn, fine, at, :] for fine in range(SUB)]
            rows_here.append(pltpu.roll(rows_here[0], LANES - 1, 1))
            for fine in range(SUB):
                face = 0.5 * (rows_here[fine] + rows_here[fine + 1])
                along[fine + 1, at, :] = face
                if fine == SUB - 1:
                    along[0, at, :] = pltpu.roll(face, 1, 1)
                lead = (self.count + turn, fine)
                cross[fine, at, :] = 0.5 * (speed[lead + (at,)] + speed[lead + (after,)])

    def update(self, src, src_at, dst, dst_at):
        along, cross, fields, across, wide = self.along, self.cross, self.fields, self.across, self.wide
        last = pl.ds(wide - SUB - 1, SUB)
        first = pl.ds(0, SUB)
        now = [[src[src_at[f], fine, first, :] for fine in range(SUB)] for f in range(fields)]
        carried = [[None] * SUB for _ in range(fields)]
        for fine in range(SUB):
            face = cross[fine, last, :]
            for f in range(fields):
                before = src[src_at[f], fine, last, :]
                carried[f][fine] = face * jnp.where(face > 0.0, before, now[f][fine])
        for step in range(across):
            at = pl.ds(step * SUB, SUB)
            after = pl.ds(step * SUB + SUB, SUB) if step < across - 1 else pl.ds(1, SUB)
            flow = []
            wrap = []
            face = along[0, at, :]
            for f in range(fields):
                above = pltpu.roll(now[f][SUB - 1], 1, 1)
                wrap.append(pltpu.roll(now[f][0], LANES - 1, 1))
                flow.append(face * jnp.where(face > 0.0, above, now[f][0]))
            for fine in range(SUB):
                down_face = along[fine + 1, at, :]
                side_face = cross[fine, at, :]
                down_pick = down_face > 0.0
                side_pick = side_face > 0.0
                for f in range(fields):
                    value = now[f][fine]
                    lower = now[f][fine + 1] if fine < SUB - 1 else wrap[f]
                    right = src[src_at[f], fine, after, :]
                    down_flow = down_face * jnp.where(down_pick, value, lower)
                    side_flow = side_face * jnp.where(side_pick, value, right)
                    dst[dst_at[f], fine, at, :] = (
                        value + (flow[f] - down_flow) + (carried[f][fine] - side_flow)
                    )
                    flow[f] = down_flow
                    carried[f][fine] = side_flow
                    now[f][fine] = right

    def run(self, turn):
        fields, across, plain = self.fields, self.across, self.plain
        tall = self.rows + 2 * NSUB
        self.faces(turn)
        mine = [field * self.count + turn for field in range(fields)]
        spare = list(range(fields))

        def pair(_, carry):
            self.update(self.here, mine, self.there, spare)
            self.update(self.there, spare, self.here, mine)
            return carry

        lax.fori_loop(0, NSUB // 2, pair, 0)
        for field in range(fields):
            lead = field * self.count + turn
            for fine in range(SUB):
                for step in range(across):
                    plain[fine, pl.ds(SUB - NSUB + step, SUB, stride=across), :] = self.here[
                        lead, fine, pl.ds(step * SUB, SUB), :
                    ]
                self.high[field, pl.ds(fine, LANES, stride=SUB), :] = plain[fine, pl.ds(SUB, LANES), :].T
            base = lead * self.size
            for level in range(self.size):
                self.raw[base + level] = self.high[field, pl.ds(level * tall + NSUB, self.rows), :]
            self.store(field, turn).start()

    def finish(self):
        for field in range(self.fields):
            for turn in range(self.count):
                self.store(field, turn).wait()


def up_kernel(
    answered_at, slots, blocks, weight, coef_c, coef_g, recip,
    out, answered, slot, block, held, made_c, made_g, made_r, sums, solved, final, sem, out_sem, *, parts
):
    share = held.shape[0] // parts
    first = [
        pltpu.make_async_copy(answered_at, answered, sem.at[0]),
        pltpu.make_async_copy(slots, slot, sem.at[1]),
        pltpu.make_async_copy(blocks, block, sem.at[2]),
    ]
    weights = [
        pltpu.make_async_copy(
            weight.at[pl.ds(part * share, share)], held.at[pl.ds(part * share, share)], sem.at[6 + part]
        )
        for part in range(parts)
    ]
    later = [
        pltpu.make_async_copy(recip, made_r, sem.at[5]),
        pltpu.make_async_copy(coef_g, made_g, sem.at[4]),
        pltpu.make_async_copy(coef_c, made_c, sem.at[3]),
    ]
    for copy in first + weights + later:
        copy.start()
    leaving = up_part(
        answered, out, slot, block, held, made_c, made_g, made_r, sums, solved, final,
        first, weights, later, out_sem,
    )
    for copy in leaving:
        copy.wait()


def up(answered, slots, blocks, weight, coef_c, coef_g, recip, levels, cap):
    fields = coef_g.shape[0]
    count = recip.shape[0]
    rows = cap * (fields + 1)
    padded = round_up(levels, SUB)
    parts = 4
    return pl.pallas_call(
        functools.partial(up_kernel, parts=parts),
        out_shape=shape((fields, levels, count * LANES)),
        in_specs=[ANY] * 7,
        out_specs=ANY,
        scratch_shapes=[
            pltpu.VMEM(answered.shape, BF16),
            pltpu.SMEM(slots.shape, jnp.int32),
            pltpu.SMEM(blocks.shape, jnp.int32),
            pltpu.VMEM(weight.shape, BF16),
            pltpu.VMEM(coef_c.shape, F32),
            pltpu.VMEM(coef_g.shape, F32),
            pltpu.VMEM(recip.shape, F32),
            pltpu.VMEM((count, rows, LANES), F32),
            pltpu.VMEM((fields, levels * count, LANES), F32),
            pltpu.VMEM((fields, padded, count * LANES), F32),
            pltpu.SemaphoreType.DMA((6 + parts,)),
            pltpu.SemaphoreType.DMA((padded // SUB,)),
        ],
        compiler_params=params(GRANT),
        cost_estimate=cost(1e7, 6e6),
        name="up_sweep",
    )(answered, slots, blocks, weight, coef_c, coef_g, recip)


def advect_kernel(
    laid, from_west, from_east, fluxes_at, answered_at, out, answered, fluxes, thin, sem, *scratch,
    fields, atm, ocn
):
    per = laid.shape[0] // (fields + 2)
    ocean = Transport(laid, from_west, from_east, out, scratch, fields, 0, per)
    smalls = [
        pltpu.make_async_copy(answered_at, answered, sem.at[0]),
        pltpu.make_async_copy(fluxes_at, fluxes, sem.at[1]),
    ]
    ocean.start(0)
    for copy in smalls:
        copy.start()
    i = lax.axis_index("atm")
    j = lax.axis_index("ocn")
    back = answered.shape[1] - round_up(fields * NSUB, 16)

    def neighbour(di, dj):
        inside = (i + di >= 0) & (i + di < atm) & (j + dj >= 0) & (j + dj < ocn)
        index = jnp.where(inside, (i + di) * ocn + j + dj, 0)
        value = answered[index, pl.ds(back, answered.shape[1] - back), :].astype(F32)
        return jnp.where(inside, value, 0.0)

    ocean.messages()
    ocean.ready(0)
    for turn in range(1, per):
        ocean.start(turn)
    for copy in smalls:
        copy.wait()
    ocean.force(neighbour, fluxes, thin)

    def body(turn, carry):
        ocean.run(turn)
        for later in range(1, per):
            pl.when(turn == later - 1)(functools.partial(ocean.ready, later))
        return carry

    lax.fori_loop(0, per, body, 0)
    ocean.finish()


def advect(laid, from_west, from_east, fluxes, answered, rows, size, atm, ocn):
    fields = fluxes.shape[0]
    per = laid.shape[0] // (fields + 2)
    return pl.pallas_call(
        functools.partial(advect_kernel, fields=fields, atm=atm, ocn=ocn),
        out_shape=shape((fields * per * size, rows, LANES)),
        in_specs=[ANY] * 5,
        out_specs=ANY,
        scratch_shapes=[
            pltpu.VMEM(answered.shape, BF16),
            pltpu.VMEM(fluxes.shape, F32),
            pltpu.VMEM((fields, SUB * SUB, LANES), F32),
            pltpu.SemaphoreType.DMA((2,)),
        ]
        + Transport.scratch(laid.shape, from_west.shape, rows, size, fields, per),
        compiler_params=params(GRANT),
        cost_estimate=cost(5e7, 1.2e7),
        name="advect",
    )(laid, from_west, from_east, fluxes, answered)


def per_device(
    atm_state,
    diffusivity,
    send_slot,
    atm_block,
    recv_row,
    remap_weight,
    ocean_tracer,
    ocean_velocity,
    exchange_coef,
    surface_kind,
    ice_surface,
):
    atm, ocn = lax.axis_size("atm"), lax.axis_size("ocn")
    owners = atm * ocn
    fields, levels, _ = atm_state.shape
    cap = recv_row.shape[1] // owners
    depth, rows, columns = ocean_tracer.shape[1:]
    most = LANES // ((rows + 2 * NSUB) // SUB)
    size = max(count for count in range(1, most + 1) if depth % count == 0)
    tracer = ocean_tracer.reshape(-1, rows, columns)
    speed = ocean_velocity.reshape(-1, rows, columns)

    def neighbours(axis):
        count = lax.axis_size(axis)
        up = [(place, place + 1) for place in range(count - 1)]
        return up, [(target, source) for source, target in up]

    forward, backward = neighbours("atm")
    first, last = row_pack(tracer, speed)
    south = lax.ppermute(first, "atm", backward)
    north = lax.ppermute(last, "atm", forward)
    coef_c, coef_g, recip, outgoing = down(
        atm_state, diffusivity, send_slot, atm_block, remap_weight, first, owners, cap
    )
    arrived = lax.all_to_all(outgoing, ("atm", "ocn"), split_axis=0, concat_axis=0, tiled=True)
    fluxes, answer = flux_step(
        arrived.reshape(-1, LANES), recv_row, exchange_coef, surface_kind, ice_surface,
        ocean_tracer, north, south, owners, atm, ocn,
    )
    answered = lax.all_to_all(answer, ("atm", "ocn"), split_axis=0, concat_axis=0, tiled=True)
    laid, to_west, to_east = relayout(tracer, speed, north, south, size)
    forward, backward = neighbours("ocn")
    from_east = lax.ppermute(to_west, "ocn", backward)
    from_west = lax.ppermute(to_east, "ocn", forward)
    atm_new = up(
        answered, send_slot, atm_block, remap_weight, coef_c, coef_g, recip, levels, cap
    )
    ocean_new = advect(laid, from_west, from_east, fluxes, answered, rows, size, atm, ocn)
    return atm_new, ocean_new.reshape(ocean_tracer.shape)


def solution(mesh):
    placed = (
        P(None, None, ("atm", "ocn")),
        P(None, ("atm", "ocn")),
        P(("atm", "ocn"), None),
        P(("atm", "ocn"), None),
        P(("atm", "ocn"), None),
        P(("atm", "ocn"), None, None),
        P(None, None, "atm", "ocn"),
        P(None, None, "atm", "ocn"),
        P("atm", "ocn"),
        P("atm", "ocn"),
        P(None, "atm", "ocn"),
    )
    return jax.shard_map(
        per_device,
        mesh=mesh,
        in_specs=placed,
        out_specs=(P(None, None, ("atm", "ocn")), P(None, None, "atm", "ocn")),
        check_vma=False,
    )
```

```python
import functools

import jax
import jax.numpy as jnp
from jax import lax
from jax.experimental import pallas as pl
from jax.experimental.pallas import tpu as pltpu
from jax.sharding import PartitionSpec as P

NSUB = 4
SUB = 8
LANES = 128
GRANT = 52
GRANT_ALL = 60
F32 = jnp.float32
BF16 = jnp.bfloat16
VMEM = pl.BlockSpec(memory_space=pltpu.VMEM)
ANY = pl.BlockSpec(memory_space=pl.ANY)


def shape(dims, kind=F32):
    return jax.ShapeDtypeStruct(dims, kind)


def round_up(value, unit):
    return -(-value // unit) * unit


def params(mib):
    return pltpu.CompilerParams(vmem_limit_bytes=mib * 2**20)


def cost(flops, moved):
    return pl.CostEstimate(flops=int(flops), bytes_accessed=int(moved), transcendentals=0)


def edge_copies(tracer, speed, head, tail, sem):
    tracer_count, rows, _ = tracer.shape
    speed_count = speed.shape[0]
    copies = []
    for place, (start, into) in enumerate(((0, head), (rows - SUB, tail))):
        copies.append(
            pltpu.make_async_copy(
                tracer.at[:, pl.ds(start, SUB), :], into.at[pl.ds(0, tracer_count)], sem.at[place, 0]
            )
        )
        copies.append(
            pltpu.make_async_copy(
                speed.at[:, pl.ds(start, SUB), :],
                into.at[pl.ds(tracer_count, speed_count)],
                sem.at[place, 1],
            )
        )
    return copies


def pack_edges(total, head, tail, first, last):
    spare = head.shape[0] - total
    for into in (head, tail):
        into[pl.ds(total, spare)] = jnp.zeros((spare, SUB, LANES), F32)
    for into, out, shift in ((head, first, 0), (tail, last, SUB - NSUB)):
        flat = into.reshape(into.shape[0] * SUB, LANES)
        for row in range(NSUB):
            for part in range(0, into.shape[0], 16):
                out[row, pl.ds(part, 16), :] = flat[
                    pl.ds(part * SUB + shift + row, 16, stride=SUB), :
                ].astype(BF16)


def down_kernel(
    profile, diffusion, slots, blocks, weight, tracer, speed, coef_c, coef_g, recip, out, first, last,
    given, mixing, slot, block, held, prof, diff, made_c, made_g, made_r, placed, total, sent, head, tail,
    sem, level_sem, edge_sem,
):
    fields, levels, columns = profile.shape
    count = columns // LANES
    width = fields + 1
    owners = out.shape[0]
    cap = out.shape[1] // width
    rows = cap * width
    lows = range(0, levels, SUB)

    def part(index):
        low = index * SUB
        deep = min(SUB, levels - low)
        return low, deep, min(SUB, levels - 1 - low)

    loads = []
    for index, low in enumerate(lows):
        low, deep, deep_k = part(index)
        pair = [
            pltpu.make_async_copy(
                diffusion.at[pl.ds(low, deep_k)], mixing.at[pl.ds(low, deep_k)], level_sem.at[index, 0]
            ),
            pltpu.make_async_copy(
                profile.at[:, pl.ds(low, deep), :], given.at[:, pl.ds(low, deep), :], level_sem.at[index, 1]
            ),
        ]
        for copy in pair:
            copy.start()
        loads.append(pair)
    others = [
        pltpu.make_async_copy(weight, held, sem.at[0]),
        pltpu.make_async_copy(slots, slot, sem.at[1]),
        pltpu.make_async_copy(blocks, block, sem.at[2]),
    ]
    edges = edge_copies(tracer, speed, head, tail, edge_sem)
    for copy in others + edges:
        copy.start()
    placed[...] = jnp.zeros(placed.shape, F32)
    total[...] = jnp.zeros(total.shape, F32)
    below = None
    for index, _ in enumerate(lows):
        low, deep, deep_k = part(index)
        for copy in loads[index]:
            copy.wait()
        for place in range(count):
            across = pl.ds(place * LANES, LANES)
            diff[pl.ds(low * count + place, deep_k, stride=count), :] = mixing[pl.ds(low, deep_k), across]
            for field in range(fields):
                prof[field, pl.ds(low * count + place, deep, stride=count), :] = given[
                    field, pl.ds(low, deep), across
                ]
        for level in range(low, low + deep):
            here = pl.ds(level * count, count)
            rhs = [prof[field, here, :] for field in range(fields)]
            bottom = jnp.full((count, LANES), 1.0, F32)
            if level < levels - 1:
                above = diff[here, :]
                bottom = bottom + above
            if level > 0:
                bottom = bottom + below * (1.0 + c_now)
                rhs = [rhs[field] + below * g_now[field] for field in range(fields)]
            inverse = 1.0 / bottom
            g_now = [value * inverse for value in rhs]
            for field in range(fields):
                made_g[field, here, :] = g_now[field]
            if level < levels - 1:
                c_now = -above * inverse
                made_c[here, :] = c_now
                below = above
    made_r[...] = inverse
    results_out = [
        pltpu.make_async_copy(made_c, coef_c, sem.at[3]),
        pltpu.make_async_copy(made_g, coef_g, sem.at[4]),
        pltpu.make_async_copy(made_r, recip, sem.at[5]),
    ]
    for copy in results_out:
        copy.start()
    for number in range(cap):
        for field, value in enumerate(g_now + [inverse]):
            placed[number, pl.ds(number * width + field, count, stride=rows), :] = value
    for copy in others:
        copy.wait()
    step = 32

    def body(group, _):
        results = []
        for inner in range(step):
            at = group * step + inner
            start = pl.multiple_of(block[0, at] * rows, rows)
            left = placed[slot[0, at] % cap, pl.ds(start, rows), :].astype(BF16)
            results.append(
                lax.dot_general(
                    left, held[at], (((1,), (1,)), ((), ())), preferred_element_type=F32
                )
            )
        for inner in range(step):
            owner = slot[0, group * step + inner] // cap
            total[owner] = total[owner] + results[inner]
        return 0

    lax.fori_loop(0, held.shape[0] // step, body, 0)
    for owner in range(owners):
        sent[owner] = total[owner].astype(BF16)
    final = pltpu.make_async_copy(sent, out, sem.at[6])
    final.start()
    for copy in edges:
        copy.wait()
    pack_edges(tracer.shape[0] + speed.shape[0], head, tail, first, last)
    for copy in results_out:
        copy.wait()
    final.wait()


def down(profile, diffusion, slots, blocks, weight, tracer, speed, owners, cap):
    fields, levels, columns = profile.shape
    count = columns // LANES
    rows = cap * (fields + 1)
    padded = round_up(levels, SUB)
    lines = round_up(tracer.shape[0] + speed.shape[0], 16)
    return pl.pallas_call(
        down_kernel,
        out_shape=(
            shape(((levels - 1) * count, LANES)),
            shape((fields, levels * count, LANES)),
            shape((count, LANES)),
            shape((owners, rows, LANES), BF16),
            shape((NSUB, lines, LANES), BF16),
            shape((NSUB, lines, LANES), BF16),
        ),
        in_specs=[ANY] * 7,
        out_specs=(ANY,) * 4 + (VMEM, VMEM),
        scratch_shapes=[
            pltpu.VMEM((fields, padded, columns), F32),
            pltpu.VMEM((padded, columns), F32),
            pltpu.SMEM(slots.shape, jnp.int32),
            pltpu.SMEM(blocks.shape, jnp.int32),
            pltpu.VMEM(weight.shape, BF16),
            pltpu.VMEM((fields, levels * count, LANES), F32),
            pltpu.VMEM(((levels - 1) * count, LANES), F32),
            pltpu.VMEM(((levels - 1) * count, LANES), F32),
            pltpu.VMEM((fields, levels * count, LANES), F32),
            pltpu.VMEM((count, LANES), F32),
            pltpu.VMEM((cap, count * rows, LANES), F32),
            pltpu.VMEM((owners, rows, LANES), F32),
            pltpu.VMEM((owners, rows, LANES), BF16),
            pltpu.VMEM((lines, SUB, LANES), F32),
            pltpu.VMEM((lines, SUB, LANES), F32),
            pltpu.SemaphoreType.DMA((7,)),
            pltpu.SemaphoreType.DMA((padded // SUB, 2)),
            pltpu.SemaphoreType.DMA((2, 2)),
        ],
        compiler_params=params(GRANT_ALL),
        cost_estimate=cost(1e7, 6e6),
        name="down_sweep",
    )(profile, diffusion, slots, blocks, weight, tracer, speed)


def flux_kernel(
    arrived_at, recv_at, coef_at, kind_at, ice_at, tracer, after, fluxes_at, answer_at,
    arrived, recv, coef, kind, ice, surface, fluxes, answer, narrow, sem, *, atm, ocn
):
    loads = [
        pltpu.make_async_copy(source, into, sem.at[place])
        for place, (source, into) in enumerate(
            (
                (recv_at, recv),
                (arrived_at, arrived),
                (coef_at, coef),
                (kind_at, kind),
                (ice_at, ice),
                (tracer.at[:, pl.ds(0, 1)], surface),
            )
        )
    ]
    for copy in loads:
        copy.start()
    fields, rows, _ = ice.shape
    width = fields + 1
    slot_total = recv.shape[1]
    owners, chunk, _ = answer.shape
    back = arrived.shape[0] // owners
    spread = (
        lax.broadcasted_iota(jnp.int32, (slot_total, slot_total * width), 1) // width
        == lax.broadcasted_iota(jnp.int32, (slot_total, slot_total * width), 0)
    ).astype(F32).astype(BF16)
    loads[0].wait()
    row_of = jnp.broadcast_to(recv[...], (SUB, slot_total)).astype(F32).astype(BF16)
    row_of = jnp.dot(row_of, spread, preferred_element_type=F32)[0:1]
    lane = lax.broadcasted_iota(jnp.int32, (1, slot_total * width), 1)
    key = row_of.astype(jnp.int32) * width + lane % width
    line = lax.broadcasted_iota(jnp.int32, (width * rows, 1), 0)
    chosen = ((line % rows) * width + line // rows == key).astype(F32)
    source = lax.broadcasted_iota(jnp.int32, (LANES, 3 * LANES), 0)
    target = lax.broadcasted_iota(jnp.int32, (LANES, 3 * LANES), 1)
    own = source + NSUB
    south = source + rows + NSUB
    north = source - (rows - NSUB)
    pos = jnp.where(target < LANES, own, jnp.where(target < 2 * LANES, south, north))
    fits = (
        ((target < LANES) & (source < rows))
        | ((target >= LANES) & (target < 2 * LANES) & (source < NSUB))
        | ((target >= 2 * LANES) & (source >= rows - NSUB) & (source < rows))
    )
    place = (fits & ((pos % SUB) * SUB + pos // SUB == target % LANES)).astype(F32).astype(BF16)
    turned = chosen.T.astype(BF16)
    chosen = chosen.astype(BF16)
    for copy in loads[1:]:
        copy.wait()
    summed = jnp.dot(chosen, arrived[...], preferred_element_type=F32)
    hold = jnp.where(kind[...] != 0, coef[...], 0.0)
    over = 1.0 + hold * summed[fields * rows : (fields + 1) * rows]
    rounded = []
    for field in range(fields):
        top = jnp.where(kind[...] == 2, ice[field], surface[field, 0])
        value = hold * (top - summed[field * rows : (field + 1) * rows]) / over
        fluxes[field] = value
        rounded.append(value.astype(BF16).astype(F32))
    stacked = jnp.concatenate(rounded + [jnp.zeros((rows, LANES), F32)], axis=0).astype(BF16)
    returned = jnp.dot(turned, stacked, preferred_element_type=F32)
    for owner in range(owners):
        answer[owner, pl.ds(0, back), :] = returned[owner * back : (owner + 1) * back]
        answer[owner, pl.ds(back, chunk - back), :] = jnp.zeros((chunk - back, LANES), F32)

    sides = []
    for field in range(fields):
        tall = jnp.concatenate([rounded[field], jnp.zeros((LANES - rows, LANES), F32)], axis=0)
        sides.append(jnp.dot(tall.T.astype(BF16), place, preferred_element_type=F32))
    gap = jnp.zeros((fields, LANES), F32)
    i = lax.axis_index("atm")
    j = lax.axis_index("ocn")
    for di in (-1, 0, 1):
        for dj in (-1, 0, 1):
            if di == 0 and dj == 0:
                continue
            pieces = []
            for field in range(fields):
                if dj == 0:
                    low = 0 if di < 0 else rows - NSUB
                    pieces.append(rounded[field][low : low + NSUB])
                else:
                    low = 0 if dj < 0 else LANES - NSUB
                    part = {0: 0, -1: 1, 1: 2}[di] * LANES
                    pieces.append(sides[field][low : low + NSUB, part : part + LANES])
            tile = jnp.concatenate(pieces, axis=0)
            most = chunk - back
            filled = []
            for row in range(most, fields * NSUB):
                filled += [gap, tile[row : row + 1]]
            filled.append(jnp.zeros((back - len(filled) // 2 * (fields + 1), LANES), F32))
            among = jnp.concatenate([part for part in filled if part.shape[0] > 0], axis=0)

            @pl.when((i + di >= 0) & (i + di < atm) & (j + dj >= 0) & (j + dj < ocn))
            def _():
                owner = (i + di) * ocn + j + dj
                answer[owner, pl.ds(back, most), :] = tile[:most]
                answer[owner, pl.ds(0, back), :] = answer[owner, pl.ds(0, back), :] + among

    flat = answer.reshape(owners * chunk, LANES)
    for part in range(0, owners * chunk, 16):
        narrow[pl.ds(part, 16), :] = flat[pl.ds(part, 16), :].astype(BF16)
    stores = [
        pltpu.make_async_copy(narrow, answer_at, sem.at[6]),
        pltpu.make_async_copy(fluxes, fluxes_at, sem.at[7]),
    ]
    for copy in stores:
        copy.start()
    for copy in stores:
        copy.wait()


def flux_step(arrived, recv, coef, kind, ice, tracer, after, owners, atm, ocn):
    fields, rows, _ = ice.shape
    back = arrived.shape[0] // owners
    chunk = back + extra_rows(fields)
    return pl.pallas_call(
        functools.partial(flux_kernel, atm=atm, ocn=ocn),
        out_shape=(shape(ice.shape), shape((owners * chunk, LANES), BF16)),
        in_specs=[ANY] * 7,
        out_specs=(ANY, ANY),
        scratch_shapes=[
            pltpu.VMEM(arrived.shape, BF16),
            pltpu.VMEM(recv.shape, jnp.int32),
            pltpu.VMEM(coef.shape, F32),
            pltpu.VMEM(kind.shape, jnp.int32),
            pltpu.VMEM(ice.shape, F32),
            pltpu.VMEM((fields, 1, rows, LANES), F32),
            pltpu.VMEM(ice.shape, F32),
            pltpu.VMEM((owners, chunk, LANES), F32),
            pltpu.VMEM((owners * chunk, LANES), BF16),
            pltpu.SemaphoreType.DMA((8,)),
        ],
        compiler_params=params(GRANT),
        cost_estimate=cost(1e7, 1e6),
        name="flux_step",
    )(arrived, recv, coef, kind, ice, tracer, after)


def extra_rows(fields):
    return round_up((fields - 1) * NSUB, SUB)


def widen(narrow, wide):
    flat = wide.reshape(wide.shape[0] * wide.shape[1], LANES)
    for part in range(0, flat.shape[0], 16):
        flat[pl.ds(part, 16), :] = narrow[pl.ds(part, 16), :].astype(F32)


def spot(column, across):
    return column % across * SUB + column // across


def relayout_kernel(tracer, speed, out, west, east, raw, tall, plain, done, fetched, stored):
    tracer_count, rows, _ = tracer.shape
    total = tracer_count + speed.shape[0]
    groups = out.shape[0]
    size = total // groups
    high = rows + 2 * NSUB
    wide = out.shape[2]
    across = wide // SUB

    for group in range(groups):
        if (group + 1) * size <= tracer_count:
            source = tracer.at[pl.ds(group * size, size)]
        else:
            source = speed.at[pl.ds(group * size - tracer_count, size)]
        pltpu.make_async_copy(source, raw.at[pl.ds(group * size, size)], fetched.at[group]).start()
    for part in range(0, tall.shape[0] // high, SUB):
        for row in list(range(NSUB)) + list(range(rows + NSUB, high)):
            tall[pl.ds(part * high + row, SUB, stride=high), :] = jnp.zeros((SUB, LANES), F32)

    def body(group, _):
        pltpu.make_async_copy(
            tracer.at[pl.ds(0, size)], raw.at[pl.ds(group * size, size)], fetched.at[group]
        ).wait()
        for level in range(size):
            tall[pl.ds(pl.multiple_of(group * size * high, SUB) + level * high + NSUB, rows), :] = raw[
                group * size + level
            ]
        for fine in range(SUB):
            stack = tall[pl.ds(group * size * high + fine, LANES, stride=SUB), :]
            plain[fine, pl.ds(SUB, LANES), :] = stack.T
            for step in range(across):
                done[group, fine, pl.ds(step * SUB, SUB), :] = plain[
                    fine, pl.ds(SUB - NSUB + step, SUB, stride=across), :
                ]
        pltpu.make_async_copy(done.at[group], out.at[group], stored.at[group]).start()
        return 0

    lax.fori_loop(0, groups, body, 0)
    slabs = groups * SUB
    flat = done.reshape(slabs * wide, LANES)
    for message, start in ((west, NSUB), (east, wide - 2 * NSUB)):
        for column in range(NSUB):
            at = spot(start + column, across)
            for part in range(0, message.shape[1], 16):
                pieces = []
                for low in (part, part + SUB):
                    if low < slabs:
                        pieces.append(flat[pl.ds(low * wide + at, SUB, stride=wide), :])
                    else:
                        pieces.append(jnp.zeros((SUB, LANES), F32))
                message[column, pl.ds(part, 16), :] = jnp.concatenate(pieces, axis=0).astype(BF16)
    for group in range(groups):
        pltpu.make_async_copy(done.at[group], out.at[group], stored.at[group]).wait()


def relayout(tracer, speed, size):
    rows = tracer.shape[1]
    total = tracer.shape[0] + speed.shape[0]
    groups = total // size
    slabs = round_up(groups * SUB, 16)
    wide = LANES + 2 * NSUB
    return pl.pallas_call(
        relayout_kernel,
        out_shape=(
            shape((groups, SUB, wide, LANES)),
            shape((NSUB, slabs, LANES), BF16),
            shape((NSUB, slabs, LANES), BF16),
        ),
        in_specs=[ANY] * 2,
        out_specs=(ANY, VMEM, VMEM),
        scratch_shapes=[
            pltpu.VMEM((total, rows, LANES), F32),
            pltpu.VMEM((round_up(total, 16) * (rows + 2 * NSUB), LANES), F32),
            pltpu.VMEM((SUB, LANES + 2 * SUB, LANES), F32),
            pltpu.VMEM((groups, SUB, wide, LANES), F32),
            pltpu.SemaphoreType.DMA((groups,)),
            pltpu.SemaphoreType.DMA((groups,)),
        ],
        compiler_params=params(GRANT),
        cost_estimate=cost(1e7, 1.4e7),
        name="relayout",
    )(tracer, speed)


def halo_kernel(
    north_at, south_at, west_at, east_at, out, west, east,
    north, south, own_west, own_east, stacks, plain, done, slim, twice, sem, stored, *, size, coarse
):
    groups = out.shape[0]
    wide = out.shape[1] // NSUB
    across = wide // SUB
    loads = [
        pltpu.make_async_copy(source, into, sem.at[place])
        for place, (source, into) in enumerate(
            ((north_at, north), (south_at, south), (west_at, own_west), (east_at, own_east))
        )
    ]
    for copy in loads:
        copy.start()
    for copy in loads:
        copy.wait()
    for row in range(NSUB):
        for part in range(0, north.shape[1], 16):
            for halo, start in ((north, 0), (south, coarse - 1)):
                stacks[row, pl.ds(part * coarse + start, 16, stride=coarse), :] = halo[
                    row, pl.ds(part, 16), :
                ].astype(F32)
    for group in range(groups):
        for row in range(NSUB):
            stack = stacks[row, pl.ds(group * size * coarse, LANES), :]
            plain[row, pl.ds(SUB, LANES), :] = stack.T
            for step in range(across):
                done[group, row, pl.ds(step * SUB, SUB), :] = plain[
                    row, pl.ds(SUB - NSUB + step, SUB, stride=across), :
                ]
        lean = done.reshape(groups, NSUB * wide, LANES)
        for part in range(0, NSUB * wide, 16):
            slim[group, pl.ds(part, 16), :] = lean[group, pl.ds(part, 16), :].astype(BF16)
        pltpu.make_async_copy(slim.at[group], out.at[group], stored.at[group]).start()
    flat = done.reshape(groups * NSUB * wide, LANES)
    line = lax.broadcasted_iota(jnp.int32, (16, LANES), 0) % SUB
    lane = lax.broadcasted_iota(jnp.int32, (16, LANES), 1) % coarse
    taken = ((line < NSUB) & (lane == 0)) | ((line >= NSUB) & (lane == coarse - 1))
    for message, own, start in ((west, own_west, NSUB), (east, own_east, wide - 2 * NSUB)):
        for column in range(NSUB):
            at = spot(start + column, across)
            for group in range(groups):
                few = flat[pl.ds(group * NSUB * wide + at, NSUB, stride=wide), :]
                twice[pl.ds(group * SUB, NSUB), :] = few
                twice[pl.ds(group * SUB + NSUB, NSUB), :] = few
            for part in range(0, message.shape[1], 16):
                here = pl.ds(part, 16)
                message[column, here, :] = jnp.where(
                    taken, twice[here, :], own[column, here, :].astype(F32)
                ).astype(BF16)
    for group in range(groups):
        pltpu.make_async_copy(slim.at[group], out.at[group], stored.at[group]).wait()


def halos(north, south, west, east, groups, size, rows):
    wide = LANES + 2 * NSUB
    coarse = (rows + 2 * NSUB) // SUB
    slabs = west.shape[1]
    return pl.pallas_call(
        functools.partial(halo_kernel, size=size, coarse=coarse),
        out_shape=(
            shape((groups, NSUB * wide, LANES), BF16),
            shape(west.shape, BF16),
            shape(east.shape, BF16),
        ),
        in_specs=[ANY] * 4,
        out_specs=(ANY, VMEM, VMEM),
        scratch_shapes=[
            pltpu.VMEM(north.shape, BF16),
            pltpu.VMEM(south.shape, BF16),
            pltpu.VMEM(west.shape, BF16),
            pltpu.VMEM(east.shape, BF16),
            pltpu.VMEM((NSUB, north.shape[1] * coarse, LANES), F32),
            pltpu.VMEM((NSUB, LANES + 2 * SUB, LANES), F32),
            pltpu.VMEM((groups, NSUB, wide, LANES), F32),
            pltpu.VMEM((groups, NSUB * wide, LANES), BF16),
            pltpu.VMEM((slabs, LANES), F32),
            pltpu.SemaphoreType.DMA((4,)),
            pltpu.SemaphoreType.DMA((groups,)),
        ],
        compiler_params=params(GRANT),
        cost_estimate=cost(1e7, 6e6),
        name="row_halos",
    )(north, south, west, east)


def up_part(
    arrived, answer, out, slot, block, held, made_c, made_g, made_r, sums, solved, final, first, weights, later, out_sem
):
    fields, levels, columns = out.shape
    count = columns // LANES
    width = fields + 1
    rows = sums.shape[1]
    cap = rows // width
    parts = len(weights)
    share = held.shape[0] // parts
    sums[...] = jnp.zeros(sums.shape, F32)
    slot_row = lax.broadcasted_iota(jnp.int32, (rows, LANES), 0) // width
    step = 32

    def body(group, _):
        results = []
        for inner in range(step):
            at = group * step + inner
            left = answer[slot[0, at] // cap, pl.ds(0, rows), :].astype(BF16)
            results.append(jnp.dot(left, held[at], preferred_element_type=F32))
        for inner in range(step):
            at = group * step + inner
            kept = jnp.where(slot_row == slot[0, at] % cap, results[inner], 0.0)
            sums[block[0, at]] = sums[block[0, at]] + kept
        return 0

    for copy in first:
        copy.wait()
    widen(arrived, answer)
    for part in range(parts):
        weights[part].wait()
        lax.fori_loop(part * share // step, (part + 1) * share // step, body, 0)
    for copy in later:
        copy.wait()
    flat = sums.reshape(count * rows, LANES)
    now = []
    last = pl.ds((levels - 1) * count, count)
    for field in range(fields):
        flux = flat[pl.ds(field, count, stride=rows), :]
        for number in range(1, cap):
            flux = flux + flat[pl.ds(number * width + field, count, stride=rows), :]
        now.append(made_g[field, last, :] + made_r[...] * flux)
        solved[field, last, :] = now[field]
    copies = []
    for low in reversed(range(0, levels, SUB)):
        deep = min(SUB, levels - low)
        for level in range(min(low + deep, levels - 1) - 1, low - 1, -1):
            here = pl.ds(level * count, count)
            for field in range(fields):
                now[field] = made_g[field, here, :] - made_c[here, :] * now[field]
                solved[field, here, :] = now[field]
        for field in range(fields):
            for place in range(count):
                final[field, pl.ds(low, deep), pl.ds(place * LANES, LANES)] = solved[
                    field, pl.ds(low * count + place, deep, stride=count), :
                ]
        copies.append(
            pltpu.make_async_copy(
                final.at[:, pl.ds(low, deep), :], out.at[:, pl.ds(low, deep), :], out_sem.at[low // SUB]
            )
        )
        copies[-1].start()
    return copies


class Transport:
    def __init__(self, laid, edge, from_west_at, from_east_at, out, scratch, fields, first, count):
        self.laid, self.edge, self.out, self.fields, self.first, self.count = laid, edge, out, fields, first, count
        (
            self.from_west, self.from_east, self.here, self.there, self.speed, self.along, self.cross,
            self.halo, self.plain, self.high, self.raw, self.edges, self.sem, self.fetched, self.stored,
        ) = scratch
        self.per = laid.shape[0] // (fields + 2)
        self.size = out.shape[0] // (fields * self.per)
        self.rows = out.shape[1]
        self.wide = laid.shape[2]
        self.across = self.wide // SUB
        self.smalls = [
            pltpu.make_async_copy(from_west_at, self.from_west, self.sem.at[0]),
            pltpu.make_async_copy(from_east_at, self.from_east, self.sem.at[1]),
        ]

    @staticmethod
    def scratch(laid_shape, message_shape, out_rows, size, fields, count):
        groups, _, wide, _ = laid_shape
        return [
            pltpu.VMEM(message_shape, BF16),
            pltpu.VMEM(message_shape, BF16),
            pltpu.VMEM((fields * count, SUB, wide, LANES), F32),
            pltpu.VMEM((fields, SUB, wide, LANES), F32),
            pltpu.VMEM((2 * count, SUB, wide, LANES), F32),
            pltpu.VMEM((SUB + 1, wide, LANES), F32),
            pltpu.VMEM((SUB, wide, LANES), F32),
            pltpu.VMEM((2,) + message_shape, F32),
            pltpu.VMEM((fields, SUB, LANES + 2 * SUB, LANES), F32),
            pltpu.VMEM((fields, SUB * LANES, LANES), F32),
            pltpu.VMEM((fields * count * size, out_rows, LANES), F32),
            pltpu.VMEM(((fields + 2) * count, NSUB * wide, LANES), BF16),
            pltpu.SemaphoreType.DMA((2,)),
            pltpu.SemaphoreType.DMA((2, fields + 2, count)),
            pltpu.SemaphoreType.DMA((fields, count)),
        ]

    def fetch(self, array, turn):
        group = array * self.per + self.first + turn
        if array < self.fields:
            into = self.here.at[array * self.count + turn]
        else:
            into = self.speed.at[(array - self.fields) * self.count + turn]
        return [
            pltpu.make_async_copy(self.laid.at[group], into, self.fetched.at[0, array, turn]),
            pltpu.make_async_copy(
                self.edge.at[group], self.edges.at[array * self.count + turn], self.fetched.at[1, array, turn]
            ),
        ]

    def store(self, field, turn):
        start = (field * self.per + self.first + turn) * self.size
        return pltpu.make_async_copy(
            self.raw.at[pl.ds((field * self.count + turn) * self.size, self.size)],
            self.out.at[pl.ds(start, self.size)],
            self.stored.at[field, turn],
        )

    def start(self, turn):
        for array in range(self.fields + 2):
            for copy in self.fetch(array, turn):
                copy.start()
        if turn == 0:
            for copy in self.smalls:
                copy.start()

    def messages(self):
        for copy in self.smalls:
            copy.wait()
        for column in range(NSUB):
            self.halo[0, column] = self.from_west[column].astype(F32)
            self.halo[1, column] = self.from_east[column].astype(F32)

    def ready(self, turn):
        wide = self.wide
        coarse = (self.rows + 2 * NSUB) // SUB
        lane = lax.broadcasted_iota(jnp.int32, (SUB, LANES), 1) % coarse
        for array in range(self.fields + 2):
            for copy in self.fetch(array, turn):
                copy.wait()
            if array < self.fields:
                ref, at = self.here, array * self.count + turn
            else:
                ref, at = self.speed, (array - self.fields) * self.count + turn
            for part in range(0, NSUB * wide, 16):
                both = self.edges[array * self.count + turn, pl.ds(part, 16), :].astype(F32)
                for half in range(2):
                    value = both[half * SUB : (half + 1) * SUB]
                    row, step = divmod(part // SUB + half, self.across)
                    tile = pl.ds(step * SUB, SUB)
                    for fine, edge in ((row, 0), (row + NSUB, coarse - 1)):
                        ref[at, fine, tile, :] = jnp.where(lane == edge, value, ref[at, fine, tile, :])
            group = array * self.per + self.first + turn
            flat = ref.reshape(ref.shape[0] * SUB * wide, LANES)
            for side in range(2):
                for column in range(NSUB):
                    to = spot(column if side == 0 else wide - NSUB + column, self.across)
                    flat[pl.ds(at * (SUB * wide) + to, SUB, stride=wide), :] = self.halo[
                        side, column, pl.ds(group * SUB, SUB), :
                    ]

    def prepare(self, neighbour, fluxes, thin):
        fields, rows, plain = self.fields, self.rows, self.plain
        thin[...] = jnp.zeros(thin.shape, F32)
        up_rows = neighbour(-1, 0)
        down_rows = neighbour(1, 0)
        for field in range(fields):
            thin[field, pl.ds(0, NSUB), :] = up_rows[field * NSUB : (field + 1) * NSUB]
            thin[field, pl.ds(NSUB, rows), :] = fluxes[field]
            thin[field, pl.ds(NSUB + rows, NSUB), :] = down_rows[field * NSUB : (field + 1) * NSUB]
        lane = lax.broadcasted_iota(jnp.int32, (fields * NSUB, LANES), 1)
        sides = [sum(neighbour(di, dj) for di in (-1, 0, 1)) for dj in (-1, 1)]
        for fine in range(SUB):
            moved = []
            for side in sides:
                turned = side if fine == 0 else pltpu.roll(side, LANES - SUB * fine, 1)
                moved.append(jnp.where(lane < SUB, turned, 0.0))
            for field in range(fields):
                few = thin[field, pl.ds(fine, SUB, stride=SUB), :]
                stack = jnp.concatenate([few, jnp.zeros((LANES - SUB, LANES), F32)], axis=0)
                plain[field, fine, pl.ds(SUB, LANES), :] = stack.T
                plain[field, fine, pl.ds(SUB - NSUB, NSUB), :] = moved[0][field * NSUB : (field + 1) * NSUB]
                plain[field, fine, pl.ds(SUB + LANES, NSUB), :] = moved[1][field * NSUB : (field + 1) * NSUB]

    def force(self):
        for field in range(self.fields):
            for fine in range(SUB):
                for step in range(self.across):
                    at = (field * self.count, fine, pl.ds(step * SUB, SUB))
                    self.here[at] = (
                        self.here[at]
                        - self.plain[field, fine, pl.ds(SUB - NSUB + step, SUB, stride=self.across), :]
                    )

    def faces(self, turn):
        speed, along, cross, across = self.speed, self.along, self.cross, self.across
        for step in range(across):
            at = pl.ds(step * SUB, SUB)
            after = pl.ds(step * SUB + SUB, SUB) if step < across - 1 else pl.ds(1, SUB)
            rows_here = [speed[turn, fine, at, :] for fine in range(SUB)]
            rows_here.append(pltpu.roll(rows_here[0], LANES - 1, 1))
            for fine in range(SUB):
                face = 0.5 * (rows_here[fine] + rows_here[fine + 1])
                along[fine + 1, at, :] = face
                if fine == SUB - 1:
                    along[0, at, :] = pltpu.roll(face, 1, 1)
                lead = (self.count + turn, fine)
                cross[fine, at, :] = 0.5 * (speed[lead + (at,)] + speed[lead + (after,)])

    def update(self, src, src_at, dst, dst_at, last_step=False):
        along, cross, fields, across, wide = self.along, self.cross, self.fields, self.across, self.wide
        last = pl.ds(wide - SUB - 1, SUB)
        first = pl.ds(0, SUB)
        now = [[src[src_at[f], fine, first, :] for fine in range(SUB)] for f in range(fields)]
        carried = [[None] * SUB for _ in range(fields)]
        for fine in range(SUB):
            face = cross[fine, last, :]
            for f in range(fields):
                before = src[src_at[f], fine, last, :]
                carried[f][fine] = face * jnp.where(face > 0.0, before, now[f][fine])
        for step in range(across):
            at = pl.ds(step * SUB, SUB)
            after = pl.ds(step * SUB + SUB, SUB) if step < across - 1 else pl.ds(1, SUB)
            flow = []
            wrap = []
            face = along[0, at, :]
            for f in range(fields):
                above = pltpu.roll(now[f][SUB - 1], 1, 1)
                wrap.append(pltpu.roll(now[f][0], LANES - 1, 1))
                flow.append(face * jnp.where(face > 0.0, above, now[f][0]))
            for fine in range(SUB):
                down_face = along[fine + 1, at, :]
                side_face = cross[fine, at, :]
                down_pick = down_face > 0.0
                side_pick = side_face > 0.0
                for f in range(fields):
                    value = now[f][fine]
                    lower = now[f][fine + 1] if fine < SUB - 1 else wrap[f]
                    right = src[src_at[f], fine, after, :]
                    down_flow = down_face * jnp.where(down_pick, value, lower)
                    side_flow = side_face * jnp.where(side_pick, value, right)
                    to = pl.ds(SUB - NSUB + step, SUB, stride=across) if last_step else at
                    dst[dst_at[f], fine, to, :] = (
                        value + (flow[f] - down_flow) + (carried[f][fine] - side_flow)
                    )
                    flow[f] = down_flow
                    carried[f][fine] = side_flow
                    now[f][fine] = right

    def run(self, turn):
        fields, across, plain = self.fields, self.across, self.plain
        tall = self.rows + 2 * NSUB
        self.faces(turn)
        mine = [field * self.count + turn for field in range(fields)]
        spare = list(range(fields))

        def pair(number, carry):
            self.update(self.here, mine, self.there, spare)

            @pl.when(number < NSUB // 2 - 1)
            def _():
                self.update(self.there, spare, self.here, mine)

            @pl.when(number == NSUB // 2 - 1)
            def _():
                self.update(self.there, spare, plain, spare, last_step=True)

            return carry

        lax.fori_loop(0, NSUB // 2, pair, 0)
        for field in range(fields):
            lead = field * self.count + turn
            for fine in range(SUB):
                self.high[field, pl.ds(fine, LANES, stride=SUB), :] = plain[
                    field, fine, pl.ds(SUB, LANES), :
                ].T
            base = lead * self.size
            for level in range(self.size):
                self.raw[base + level] = self.high[field, pl.ds(level * tall + NSUB, self.rows), :]
            self.store(field, turn).start()

    def finish(self):
        for field in range(self.fields):
            for turn in range(self.count):
                self.store(field, turn).wait()


def up_kernel(
    answered_at, slots, blocks, weight, coef_c, coef_g, recip,
    out, arrived, answered, slot, block, held, made_c, made_g, made_r, sums, solved, final, sem, out_sem, *, parts
):
    share = held.shape[0] // parts
    first = [
        pltpu.make_async_copy(answered_at, arrived, sem.at[0]),
        pltpu.make_async_copy(slots, slot, sem.at[1]),
        pltpu.make_async_copy(blocks, block, sem.at[2]),
    ]
    weights = [
        pltpu.make_async_copy(
            weight.at[pl.ds(part * share, share)], held.at[pl.ds(part * share, share)], sem.at[6 + part]
        )
        for part in range(parts)
    ]
    later = [
        pltpu.make_async_copy(recip, made_r, sem.at[5]),
        pltpu.make_async_copy(coef_g, made_g, sem.at[4]),
        pltpu.make_async_copy(coef_c, made_c, sem.at[3]),
    ]
    for copy in first + weights + later:
        copy.start()
    leaving = up_part(
        arrived, answered, out, slot, block, held, made_c, made_g, made_r, sums, solved, final,
        first, weights, later, out_sem,
    )
    for copy in leaving:
        copy.wait()


def up(answered, slots, blocks, weight, coef_c, coef_g, recip, levels, cap, owners):
    fields = coef_g.shape[0]
    count = recip.shape[0]
    rows = cap * (fields + 1)
    padded = round_up(levels, SUB)
    parts = 4
    return pl.pallas_call(
        functools.partial(up_kernel, parts=parts),
        out_shape=shape((fields, levels, count * LANES)),
        in_specs=[ANY] * 7,
        out_specs=ANY,
        scratch_shapes=[
            pltpu.VMEM(answered.shape, BF16),
            pltpu.VMEM((owners, answered.shape[0] // owners, LANES), F32),
            pltpu.SMEM(slots.shape, jnp.int32),
            pltpu.SMEM(blocks.shape, jnp.int32),
            pltpu.VMEM(weight.shape, BF16),
            pltpu.VMEM(coef_c.shape, F32),
            pltpu.VMEM(coef_g.shape, F32),
            pltpu.VMEM(recip.shape, F32),
            pltpu.VMEM((count, rows, LANES), F32),
            pltpu.VMEM((fields, levels * count, LANES), F32),
            pltpu.VMEM((fields, padded, count * LANES), F32),
            pltpu.SemaphoreType.DMA((6 + parts,)),
            pltpu.SemaphoreType.DMA((padded // SUB,)),
        ],
        compiler_params=params(GRANT),
        cost_estimate=cost(1e7, 6e6),
        name="up_sweep",
    )(answered, slots, blocks, weight, coef_c, coef_g, recip)


def advect_kernel(
    laid, edge, from_west, from_east, fluxes_at, answered_at, out, arrived, answered, fluxes, thin, sem, *scratch,
    fields, atm, ocn
):
    per = laid.shape[0] // (fields + 2)
    ocean = Transport(laid, edge, from_west, from_east, out, scratch, fields, 0, per)
    smalls = [
        pltpu.make_async_copy(answered_at, arrived, sem.at[0]),
        pltpu.make_async_copy(fluxes_at, fluxes, sem.at[1]),
    ]
    ocean.start(0)
    for copy in smalls:
        copy.start()
    i = lax.axis_index("atm")
    j = lax.axis_index("ocn")

    def neighbour(di, dj):
        inside = (i + di >= 0) & (i + di < atm) & (j + dj >= 0) & (j + dj < ocn)
        index = jnp.where(inside, (i + di) * ocn + j + dj, 0)
        value = answered[index]
        width = fields + 1
        back = answered.shape[1] - extra_rows(fields)
        spare = [value[row : row + 1] for row in range(width - 1, back, width)]
        value = jnp.concatenate([value[back:]] + spare, axis=0)
        return jnp.where(inside, value, 0.0)

    for copy in smalls:
        copy.wait()
    widen(arrived, answered)
    ocean.prepare(neighbour, fluxes, thin)
    ocean.messages()
    ocean.ready(0)
    for turn in range(1, per):
        ocean.start(turn)
    ocean.force()

    def body(turn, carry):
        ocean.run(turn)
        for later in range(1, per):
            pl.when(turn == later - 1)(functools.partial(ocean.ready, later))
        return carry

    lax.fori_loop(0, per, body, 0)
    ocean.finish()


def advect(laid, edge, from_west, from_east, fluxes, answered, rows, size, atm, ocn):
    fields = fluxes.shape[0]
    per = laid.shape[0] // (fields + 2)
    return pl.pallas_call(
        functools.partial(advect_kernel, fields=fields, atm=atm, ocn=ocn),
        out_shape=shape((fields * per * size, rows, LANES)),
        in_specs=[ANY] * 6,
        out_specs=ANY,
        scratch_shapes=[
            pltpu.VMEM(answered.shape, BF16),
            pltpu.VMEM((atm * ocn, answered.shape[0] // (atm * ocn), LANES), F32),
            pltpu.VMEM(fluxes.shape, F32),
            pltpu.VMEM((fields, SUB * SUB, LANES), F32),
            pltpu.SemaphoreType.DMA((2,)),
        ]
        + Transport.scratch(laid.shape, from_west.shape, rows, size, fields, per),
        compiler_params=params(GRANT),
        cost_estimate=cost(5e7, 1.2e7),
        name="advect",
    )(laid, edge, from_west, from_east, fluxes, answered)


def per_device(
    atm_state,
    diffusivity,
    send_slot,
    atm_block,
    recv_row,
    remap_weight,
    ocean_tracer,
    ocean_velocity,
    exchange_coef,
    surface_kind,
    ice_surface,
):
    atm, ocn = lax.axis_size("atm"), lax.axis_size("ocn")
    owners = atm * ocn
    fields, levels, _ = atm_state.shape
    cap = recv_row.shape[1] // owners
    depth, rows, columns = ocean_tracer.shape[1:]
    most = LANES // ((rows + 2 * NSUB) // SUB)
    size = max(count for count in range(1, most + 1) if depth % count == 0)
    tracer = ocean_tracer.reshape(-1, rows, columns)
    speed = ocean_velocity.reshape(-1, rows, columns)

    def neighbours(axis):
        count = lax.axis_size(axis)
        up = [(place, place + 1) for place in range(count - 1)]
        return up, [(target, source) for source, target in up]

    forward, backward = neighbours("atm")
    coef_c, coef_g, recip, outgoing, first, last = down(
        atm_state, diffusivity, send_slot, atm_block, remap_weight, tracer, speed, owners, cap
    )
    south = lax.ppermute(first, "atm", backward)
    north = lax.ppermute(last, "atm", forward)
    arrived = lax.all_to_all(outgoing, ("atm", "ocn"), split_axis=0, concat_axis=0, tiled=True)
    laid, own_west, own_east = relayout(tracer, speed, size)
    fluxes, answer = flux_step(
        arrived.reshape(-1, LANES), recv_row, exchange_coef, surface_kind, ice_surface,
        ocean_tracer, own_west, owners, atm, ocn,
    )
    answered = lax.all_to_all(answer, ("atm", "ocn"), split_axis=0, concat_axis=0, tiled=True)
    edge, to_west, to_east = halos(north, south, own_west, own_east, laid.shape[0], size, rows)
    forward, backward = neighbours("ocn")
    from_east = lax.ppermute(to_west, "ocn", backward)
    from_west = lax.ppermute(to_east, "ocn", forward)
    atm_new = up(
        answered, send_slot, atm_block, remap_weight, coef_c, coef_g, recip, levels, cap, owners
    )
    ocean_new = advect(
        laid, edge, from_west, from_east, fluxes, answered, rows, size, atm, ocn
    )
    return atm_new, ocean_new.reshape(ocean_tracer.shape)


def solution(mesh):
    placed = (
        P(None, None, ("atm", "ocn")),
        P(None, ("atm", "ocn")),
        P(("atm", "ocn"), None),
        P(("atm", "ocn"), None),
        P(("atm", "ocn"), None),
        P(("atm", "ocn"), None, None),
        P(None, None, "atm", "ocn"),
        P(None, None, "atm", "ocn"),
        P("atm", "ocn"),
        P("atm", "ocn"),
        P(None, "atm", "ocn"),
    )
    return jax.shard_map(
        per_device,
        mesh=mesh,
        in_specs=placed,
        out_specs=(P(None, None, ("atm", "ocn")), P(None, None, "atm", "ocn")),
        check_vma=False,
    )
```

```python
import functools

import jax
import jax.numpy as jnp
from jax import lax
from jax.experimental import pallas as pl
from jax.experimental.pallas import tpu as pltpu
from jax.sharding import PartitionSpec as P

NSUB = 4
SUB = 8
LANES = 128
GRANT = 52
GRANT_ALL = 60
F32 = jnp.float32
BF16 = jnp.bfloat16
VMEM = pl.BlockSpec(memory_space=pltpu.VMEM)
ANY = pl.BlockSpec(memory_space=pl.ANY)


def shape(dims, kind=F32):
    return jax.ShapeDtypeStruct(dims, kind)


def round_up(value, unit):
    return -(-value // unit) * unit


def params(mib):
    return pltpu.CompilerParams(vmem_limit_bytes=mib * 2**20)


def cost(flops, moved):
    return pl.CostEstimate(flops=int(flops), bytes_accessed=int(moved), transcendentals=0)


def edge_copies(tracer, speed, head, tail, sem):
    tracer_count, rows, _ = tracer.shape
    speed_count = speed.shape[0]
    copies = []
    for place, (start, into) in enumerate(((0, head), (rows - SUB, tail))):
        copies.append(
            pltpu.make_async_copy(
                tracer.at[:, pl.ds(start, SUB), :], into.at[pl.ds(0, tracer_count)], sem.at[place, 0]
            )
        )
        copies.append(
            pltpu.make_async_copy(
                speed.at[:, pl.ds(start, SUB), :],
                into.at[pl.ds(tracer_count, speed_count)],
                sem.at[place, 1],
            )
        )
    return copies


def pack_edges(total, head, tail, first, last):
    spare = head.shape[0] - total
    for into in (head, tail):
        into[pl.ds(total, spare)] = jnp.zeros((spare, SUB, LANES), F32)
    for into, out, shift in ((head, first, 0), (tail, last, SUB - NSUB)):
        flat = into.reshape(into.shape[0] * SUB, LANES)
        for row in range(NSUB):
            for part in range(0, into.shape[0], 16):
                out[row, pl.ds(part, 16), :] = flat[
                    pl.ds(part * SUB + shift + row, 16, stride=SUB), :
                ].astype(BF16)


def down_kernel(
    profile, diffusion, slots, blocks, weight, tracer, speed, coef_c, coef_g, recip, out, first, last,
    given, mixing, slot, block, held, prof, diff, made_c, made_g, made_r, placed, total, sent, head, tail,
    sem, level_sem, edge_sem,
):
    fields, levels, columns = profile.shape
    count = columns // LANES
    width = fields + 1
    owners = out.shape[0]
    cap = out.shape[1] // width
    rows = cap * width
    lows = range(0, levels, SUB)

    def part(index):
        low = index * SUB
        deep = min(SUB, levels - low)
        return low, deep, min(SUB, levels - 1 - low)

    loads = []
    for index, low in enumerate(lows):
        low, deep, deep_k = part(index)
        pair = [
            pltpu.make_async_copy(
                diffusion.at[pl.ds(low, deep_k)], mixing.at[pl.ds(low, deep_k)], level_sem.at[index, 0]
            ),
            pltpu.make_async_copy(
                profile.at[:, pl.ds(low, deep), :], given.at[:, pl.ds(low, deep), :], level_sem.at[index, 1]
            ),
        ]
        for copy in pair:
            copy.start()
        loads.append(pair)
    others = [
        pltpu.make_async_copy(weight, held, sem.at[0]),
        pltpu.make_async_copy(slots, slot, sem.at[1]),
        pltpu.make_async_copy(blocks, block, sem.at[2]),
    ]
    edges = edge_copies(tracer, speed, head, tail, edge_sem)
    for copy in others + edges:
        copy.start()
    placed[...] = jnp.zeros(placed.shape, F32)
    total[...] = jnp.zeros(total.shape, F32)
    below = None
    for index, _ in enumerate(lows):
        low, deep, deep_k = part(index)
        for copy in loads[index]:
            copy.wait()
        for place in range(count):
            across = pl.ds(place * LANES, LANES)
            diff[pl.ds(low * count + place, deep_k, stride=count), :] = mixing[pl.ds(low, deep_k), across]
            for field in range(fields):
                prof[field, pl.ds(low * count + place, deep, stride=count), :] = given[
                    field, pl.ds(low, deep), across
                ]
        for level in range(low, low + deep):
            here = pl.ds(level * count, count)
            rhs = [prof[field, here, :] for field in range(fields)]
            bottom = jnp.full((count, LANES), 1.0, F32)
            if level < levels - 1:
                above = diff[here, :]
                bottom = bottom + above
            if level > 0:
                bottom = bottom + below * (1.0 + c_now)
                rhs = [rhs[field] + below * g_now[field] for field in range(fields)]
            inverse = 1.0 / bottom
            g_now = [value * inverse for value in rhs]
            for field in range(fields):
                made_g[field, here, :] = g_now[field]
            if level < levels - 1:
                c_now = -above * inverse
                made_c[here, :] = c_now
                below = above
    made_r[...] = inverse
    results_out = [
        pltpu.make_async_copy(made_c, coef_c, sem.at[3]),
        pltpu.make_async_copy(made_g, coef_g, sem.at[4]),
        pltpu.make_async_copy(made_r, recip, sem.at[5]),
    ]
    for copy in results_out:
        copy.start()
    for number in range(cap):
        for field, value in enumerate(g_now + [inverse]):
            placed[number, pl.ds(number * width + field, count, stride=rows), :] = value
    for copy in others:
        copy.wait()
    step = 32

    def body(group, _):
        results = []
        for inner in range(step):
            at = group * step + inner
            start = pl.multiple_of(block[0, at] * rows, rows)
            left = placed[slot[0, at] % cap, pl.ds(start, rows), :].astype(BF16)
            results.append(
                lax.dot_general(
                    left, held[at], (((1,), (1,)), ((), ())), preferred_element_type=F32
                )
            )
        for inner in range(step):
            owner = slot[0, group * step + inner] // cap
            total[owner] = total[owner] + results[inner]
        return 0

    lax.fori_loop(0, held.shape[0] // step, body, 0)
    for owner in range(owners):
        sent[owner] = total[owner].astype(BF16)
    final = pltpu.make_async_copy(sent, out, sem.at[6])
    final.start()
    for copy in edges:
        copy.wait()
    pack_edges(tracer.shape[0] + speed.shape[0], head, tail, first, last)
    for copy in results_out:
        copy.wait()
    final.wait()


def down(profile, diffusion, slots, blocks, weight, tracer, speed, owners, cap):
    fields, levels, columns = profile.shape
    count = columns // LANES
    rows = cap * (fields + 1)
    padded = round_up(levels, SUB)
    lines = round_up(tracer.shape[0] + speed.shape[0], 16)
    return pl.pallas_call(
        down_kernel,
        out_shape=(
            shape(((levels - 1) * count, LANES)),
            shape((fields, levels * count, LANES)),
            shape((count, LANES)),
            shape((owners, rows, LANES), BF16),
            shape((NSUB, lines, LANES), BF16),
            shape((NSUB, lines, LANES), BF16),
        ),
        in_specs=[ANY] * 7,
        out_specs=(ANY,) * 4 + (VMEM, VMEM),
        scratch_shapes=[
            pltpu.VMEM((fields, padded, columns), F32),
            pltpu.VMEM((padded, columns), F32),
            pltpu.SMEM(slots.shape, jnp.int32),
            pltpu.SMEM(blocks.shape, jnp.int32),
            pltpu.VMEM(weight.shape, BF16),
            pltpu.VMEM((fields, levels * count, LANES), F32),
            pltpu.VMEM(((levels - 1) * count, LANES), F32),
            pltpu.VMEM(((levels - 1) * count, LANES), F32),
            pltpu.VMEM((fields, levels * count, LANES), F32),
            pltpu.VMEM((count, LANES), F32),
            pltpu.VMEM((cap, count * rows, LANES), F32),
            pltpu.VMEM((owners, rows, LANES), F32),
            pltpu.VMEM((owners, rows, LANES), BF16),
            pltpu.VMEM((lines, SUB, LANES), F32),
            pltpu.VMEM((lines, SUB, LANES), F32),
            pltpu.SemaphoreType.DMA((7,)),
            pltpu.SemaphoreType.DMA((padded // SUB, 2)),
            pltpu.SemaphoreType.DMA((2, 2)),
        ],
        compiler_params=params(GRANT_ALL),
        cost_estimate=cost(1e7, 6e6),
        name="down_sweep",
    )(profile, diffusion, slots, blocks, weight, tracer, speed)


def flux_kernel(
    arrived_at, recv_at, coef_at, kind_at, ice_at, tracer, after, later, fluxes_at, answer_at,
    arrived, recv, coef, kind, ice, surface, fluxes, answer, narrow, sem, *, atm, ocn
):
    loads = [
        pltpu.make_async_copy(source, into, sem.at[place])
        for place, (source, into) in enumerate(
            (
                (recv_at, recv),
                (arrived_at, arrived),
                (coef_at, coef),
                (kind_at, kind),
                (ice_at, ice),
                (tracer.at[:, pl.ds(0, 1)], surface),
            )
        )
    ]
    for copy in loads:
        copy.start()
    fields, rows, _ = ice.shape
    width = fields + 1
    slot_total = recv.shape[1]
    owners, chunk, _ = answer.shape
    back = arrived.shape[0] // owners
    spread = (
        lax.broadcasted_iota(jnp.int32, (slot_total, slot_total * width), 1) // width
        == lax.broadcasted_iota(jnp.int32, (slot_total, slot_total * width), 0)
    ).astype(F32).astype(BF16)
    loads[0].wait()
    row_of = jnp.broadcast_to(recv[...], (SUB, slot_total)).astype(F32).astype(BF16)
    row_of = jnp.dot(row_of, spread, preferred_element_type=F32)[0:1]
    lane = lax.broadcasted_iota(jnp.int32, (1, slot_total * width), 1)
    key = row_of.astype(jnp.int32) * width + lane % width
    line = lax.broadcasted_iota(jnp.int32, (width * rows, 1), 0)
    chosen = ((line % rows) * width + line // rows == key).astype(F32)
    source = lax.broadcasted_iota(jnp.int32, (LANES, 3 * LANES), 0)
    target = lax.broadcasted_iota(jnp.int32, (LANES, 3 * LANES), 1)
    own = source + NSUB
    south = source + rows + NSUB
    north = source - (rows - NSUB)
    pos = jnp.where(target < LANES, own, jnp.where(target < 2 * LANES, south, north))
    fits = (
        ((target < LANES) & (source < rows))
        | ((target >= LANES) & (target < 2 * LANES) & (source < NSUB))
        | ((target >= 2 * LANES) & (source >= rows - NSUB) & (source < rows))
    )
    place = (fits & ((pos % SUB) * SUB + pos // SUB == target % LANES)).astype(F32).astype(BF16)
    turned = chosen.T.astype(BF16)
    chosen = chosen.astype(BF16)
    for copy in loads[1:]:
        copy.wait()
    summed = jnp.dot(chosen, arrived[...], preferred_element_type=F32)
    hold = jnp.where(kind[...] != 0, coef[...], 0.0)
    over = 1.0 + hold * summed[fields * rows : (fields + 1) * rows]
    rounded = []
    for field in range(fields):
        top = jnp.where(kind[...] == 2, ice[field], surface[field, 0])
        value = hold * (top - summed[field * rows : (field + 1) * rows]) / over
        fluxes[field] = value
        rounded.append(value.astype(BF16).astype(F32))
    stacked = jnp.concatenate(rounded + [jnp.zeros((rows, LANES), F32)], axis=0).astype(BF16)
    returned = jnp.dot(turned, stacked, preferred_element_type=F32)
    for owner in range(owners):
        answer[owner, pl.ds(0, back), :] = returned[owner * back : (owner + 1) * back]
        answer[owner, pl.ds(back, chunk - back), :] = jnp.zeros((chunk - back, LANES), F32)

    sides = []
    for field in range(fields):
        tall = jnp.concatenate([rounded[field], jnp.zeros((LANES - rows, LANES), F32)], axis=0)
        sides.append(jnp.dot(tall.T.astype(BF16), place, preferred_element_type=F32))
    gap = jnp.zeros((fields, LANES), F32)
    i = lax.axis_index("atm")
    j = lax.axis_index("ocn")
    for di in (-1, 0, 1):
        for dj in (-1, 0, 1):
            if di == 0 and dj == 0:
                continue
            pieces = []
            for field in range(fields):
                if dj == 0:
                    low = 0 if di < 0 else rows - NSUB
                    pieces.append(rounded[field][low : low + NSUB])
                else:
                    low = 0 if dj < 0 else LANES - NSUB
                    part = {0: 0, -1: 1, 1: 2}[di] * LANES
                    pieces.append(sides[field][low : low + NSUB, part : part + LANES])
            tile = jnp.concatenate(pieces, axis=0)
            most = chunk - back
            filled = []
            for row in range(most, fields * NSUB):
                filled += [gap, tile[row : row + 1]]
            filled.append(jnp.zeros((back - len(filled) // 2 * (fields + 1), LANES), F32))
            among = jnp.concatenate([part for part in filled if part.shape[0] > 0], axis=0)

            @pl.when((i + di >= 0) & (i + di < atm) & (j + dj >= 0) & (j + dj < ocn))
            def _():
                owner = (i + di) * ocn + j + dj
                answer[owner, pl.ds(back, most), :] = tile[:most]
                answer[owner, pl.ds(0, back), :] = answer[owner, pl.ds(0, back), :] + among

    flat = answer.reshape(owners * chunk, LANES)
    for part in range(0, owners * chunk, 16):
        narrow[pl.ds(part, 16), :] = flat[pl.ds(part, 16), :].astype(BF16)
    stores = [
        pltpu.make_async_copy(narrow, answer_at, sem.at[6]),
        pltpu.make_async_copy(fluxes, fluxes_at, sem.at[7]),
    ]
    for copy in stores:
        copy.start()
    for copy in stores:
        copy.wait()


def flux_step(arrived, recv, coef, kind, ice, tracer, after, later, owners, atm, ocn):
    fields, rows, _ = ice.shape
    back = arrived.shape[0] // owners
    chunk = back + extra_rows(fields)
    return pl.pallas_call(
        functools.partial(flux_kernel, atm=atm, ocn=ocn),
        out_shape=(shape(ice.shape), shape((owners * chunk, LANES), BF16)),
        in_specs=[ANY] * 8,
        out_specs=(ANY, ANY),
        scratch_shapes=[
            pltpu.VMEM(arrived.shape, BF16),
            pltpu.VMEM(recv.shape, jnp.int32),
            pltpu.VMEM(coef.shape, F32),
            pltpu.VMEM(kind.shape, jnp.int32),
            pltpu.VMEM(ice.shape, F32),
            pltpu.VMEM((fields, 1, rows, LANES), F32),
            pltpu.VMEM(ice.shape, F32),
            pltpu.VMEM((owners, chunk, LANES), F32),
            pltpu.VMEM((owners * chunk, LANES), BF16),
            pltpu.SemaphoreType.DMA((8,)),
        ],
        compiler_params=params(GRANT),
        cost_estimate=cost(1e7, 1e6),
        name="flux_step",
    )(arrived, recv, coef, kind, ice, tracer, after, later)


def extra_rows(fields):
    return round_up((fields - 1) * NSUB, SUB)


def widen(narrow, wide):
    flat = wide.reshape(wide.shape[0] * wide.shape[1], LANES)
    for part in range(0, flat.shape[0], 16):
        flat[pl.ds(part, 16), :] = narrow[pl.ds(part, 16), :].astype(F32)


def spot(column, across):
    return column % across * SUB + column // across


def relayout_kernel(tracer, speed, out, west, east, raw, tall, plain, done, fetched, stored):
    tracer_count, rows, _ = tracer.shape
    total = tracer_count + speed.shape[0]
    groups = out.shape[0]
    size = total // groups
    high = rows + 2 * NSUB
    wide = out.shape[2]
    across = wide // SUB

    for group in range(groups):
        if (group + 1) * size <= tracer_count:
            source = tracer.at[pl.ds(group * size, size)]
        else:
            source = speed.at[pl.ds(group * size - tracer_count, size)]
        pltpu.make_async_copy(source, raw.at[pl.ds(group * size, size)], fetched.at[group]).start()
    for part in range(0, tall.shape[0] // high, SUB):
        for row in list(range(NSUB)) + list(range(rows + NSUB, high)):
            tall[pl.ds(part * high + row, SUB, stride=high), :] = jnp.zeros((SUB, LANES), F32)

    def body(group, _):
        pltpu.make_async_copy(
            tracer.at[pl.ds(0, size)], raw.at[pl.ds(group * size, size)], fetched.at[group]
        ).wait()
        for level in range(size):
            tall[pl.ds(pl.multiple_of(group * size * high, SUB) + level * high + NSUB, rows), :] = raw[
                group * size + level
            ]
        for fine in range(SUB):
            stack = tall[pl.ds(group * size * high + fine, LANES, stride=SUB), :]
            plain[fine, pl.ds(SUB, LANES), :] = stack.T
            for step in range(across):
                done[group, fine, pl.ds(step * SUB, SUB), :] = plain[
                    fine, pl.ds(SUB - NSUB + step, SUB, stride=across), :
                ]
        pltpu.make_async_copy(done.at[group], out.at[group], stored.at[group]).start()
        return 0

    lax.fori_loop(0, groups, body, 0)
    slabs = groups * SUB
    flat = done.reshape(slabs * wide, LANES)
    for message, start in ((west, NSUB), (east, wide - 2 * NSUB)):
        for column in range(NSUB):
            at = spot(start + column, across)
            for part in range(0, message.shape[1], 16):
                pieces = []
                for low in (part, part + SUB):
                    if low < slabs:
                        pieces.append(flat[pl.ds(low * wide + at, SUB, stride=wide), :])
                    else:
                        pieces.append(jnp.zeros((SUB, LANES), F32))
                message[column, pl.ds(part, 16), :] = jnp.concatenate(pieces, axis=0).astype(BF16)
    for group in range(groups):
        pltpu.make_async_copy(done.at[group], out.at[group], stored.at[group]).wait()


def relayout(tracer, speed, size):
    rows = tracer.shape[1]
    total = tracer.shape[0] + speed.shape[0]
    groups = total // size
    slabs = round_up(groups * SUB, 16)
    wide = LANES + 2 * NSUB
    return pl.pallas_call(
        relayout_kernel,
        out_shape=(
            shape((groups, SUB, wide, LANES)),
            shape((NSUB, slabs, LANES), BF16),
            shape((NSUB, slabs, LANES), BF16),
        ),
        in_specs=[ANY] * 2,
        out_specs=(ANY, VMEM, VMEM),
        scratch_shapes=[
            pltpu.VMEM((total, rows, LANES), F32),
            pltpu.VMEM((round_up(total, 16) * (rows + 2 * NSUB), LANES), F32),
            pltpu.VMEM((SUB, LANES + 2 * SUB, LANES), F32),
            pltpu.VMEM((groups, SUB, wide, LANES), F32),
            pltpu.SemaphoreType.DMA((groups,)),
            pltpu.SemaphoreType.DMA((groups,)),
        ],
        compiler_params=params(GRANT),
        cost_estimate=cost(1e7, 1.4e7),
        name="relayout",
    )(tracer, speed)


def halo_kernel(
    north_at, south_at, west_at, east_at, out, west, east,
    north, south, own_west, own_east, stacks, plain, done, slim, twice, sem, stored, *, size, coarse
):
    groups = out.shape[0]
    wide = out.shape[1] // NSUB
    across = wide // SUB
    loads = [
        pltpu.make_async_copy(source, into, sem.at[place])
        for place, (source, into) in enumerate(
            ((north_at, north), (south_at, south), (west_at, own_west), (east_at, own_east))
        )
    ]
    for copy in loads:
        copy.start()
    for copy in loads:
        copy.wait()
    for row in range(NSUB):
        for part in range(0, north.shape[1], 16):
            for halo, start in ((north, 0), (south, coarse - 1)):
                stacks[row, pl.ds(part * coarse + start, 16, stride=coarse), :] = halo[
                    row, pl.ds(part, 16), :
                ].astype(F32)
    for group in range(groups):
        for row in range(NSUB):
            stack = stacks[row, pl.ds(group * size * coarse, LANES), :]
            plain[row, pl.ds(SUB, LANES), :] = stack.T
            for step in range(across):
                done[group, row, pl.ds(step * SUB, SUB), :] = plain[
                    row, pl.ds(SUB - NSUB + step, SUB, stride=across), :
                ]
        lean = done.reshape(groups, NSUB * wide, LANES)
        for part in range(0, NSUB * wide, 16):
            slim[group, pl.ds(part, 16), :] = lean[group, pl.ds(part, 16), :].astype(BF16)
        pltpu.make_async_copy(slim.at[group], out.at[group], stored.at[group]).start()
    flat = done.reshape(groups * NSUB * wide, LANES)
    line = lax.broadcasted_iota(jnp.int32, (16, LANES), 0) % SUB
    lane = lax.broadcasted_iota(jnp.int32, (16, LANES), 1) % coarse
    taken = ((line < NSUB) & (lane == 0)) | ((line >= NSUB) & (lane == coarse - 1))
    for message, own, start in ((west, own_west, NSUB), (east, own_east, wide - 2 * NSUB)):
        for column in range(NSUB):
            at = spot(start + column, across)
            for group in range(groups):
                few = flat[pl.ds(group * NSUB * wide + at, NSUB, stride=wide), :]
                twice[pl.ds(group * SUB, NSUB), :] = few
                twice[pl.ds(group * SUB + NSUB, NSUB), :] = few
            for part in range(0, message.shape[1], 16):
                here = pl.ds(part, 16)
                message[column, here, :] = jnp.where(
                    taken, twice[here, :], own[column, here, :].astype(F32)
                ).astype(BF16)
    for group in range(groups):
        pltpu.make_async_copy(slim.at[group], out.at[group], stored.at[group]).wait()


def halos(north, south, west, east, groups, size, rows):
    wide = LANES + 2 * NSUB
    coarse = (rows + 2 * NSUB) // SUB
    slabs = west.shape[1]
    return pl.pallas_call(
        functools.partial(halo_kernel, size=size, coarse=coarse),
        out_shape=(
            shape((groups, NSUB * wide, LANES), BF16),
            shape(west.shape, BF16),
            shape(east.shape, BF16),
        ),
        in_specs=[ANY] * 4,
        out_specs=(ANY, VMEM, VMEM),
        scratch_shapes=[
            pltpu.VMEM(north.shape, BF16),
            pltpu.VMEM(south.shape, BF16),
            pltpu.VMEM(west.shape, BF16),
            pltpu.VMEM(east.shape, BF16),
            pltpu.VMEM((NSUB, north.shape[1] * coarse, LANES), F32),
            pltpu.VMEM((NSUB, LANES + 2 * SUB, LANES), F32),
            pltpu.VMEM((groups, NSUB, wide, LANES), F32),
            pltpu.VMEM((groups, NSUB * wide, LANES), BF16),
            pltpu.VMEM((slabs, LANES), F32),
            pltpu.SemaphoreType.DMA((4,)),
            pltpu.SemaphoreType.DMA((groups,)),
        ],
        compiler_params=params(GRANT),
        cost_estimate=cost(1e7, 6e6),
        name="row_halos",
    )(north, south, west, east)


def up_part(
    arrived, answer, out, slot, block, held, made_c, made_g, made_r, sums, solved, final, first, weights, later, out_sem
):
    fields, levels, columns = out.shape
    count = columns // LANES
    width = fields + 1
    rows = sums.shape[1]
    cap = rows // width
    parts = len(weights)
    share = held.shape[0] // parts
    sums[...] = jnp.zeros(sums.shape, F32)
    slot_row = lax.broadcasted_iota(jnp.int32, (rows, LANES), 0) // width
    step = 32

    def body(group, _):
        results = []
        for inner in range(step):
            at = group * step + inner
            left = answer[slot[0, at] // cap, pl.ds(0, rows), :].astype(BF16)
            results.append(jnp.dot(left, held[at], preferred_element_type=F32))
        for inner in range(step):
            at = group * step + inner
            kept = jnp.where(slot_row == slot[0, at] % cap, results[inner], 0.0)
            sums[block[0, at]] = sums[block[0, at]] + kept
        return 0

    for copy in first:
        copy.wait()
    widen(arrived, answer)
    for part in range(parts):
        weights[part].wait()
        lax.fori_loop(part * share // step, (part + 1) * share // step, body, 0)
    for copy in later:
        copy.wait()
    flat = sums.reshape(count * rows, LANES)
    now = []
    last = pl.ds((levels - 1) * count, count)
    for field in range(fields):
        flux = flat[pl.ds(field, count, stride=rows), :]
        for number in range(1, cap):
            flux = flux + flat[pl.ds(number * width + field, count, stride=rows), :]
        now.append(made_g[field, last, :] + made_r[...] * flux)
        solved[field, last, :] = now[field]
    copies = []
    for low in reversed(range(0, levels, SUB)):
        deep = min(SUB, levels - low)
        for level in range(min(low + deep, levels - 1) - 1, low - 1, -1):
            here = pl.ds(level * count, count)
            for field in range(fields):
                now[field] = made_g[field, here, :] - made_c[here, :] * now[field]
                solved[field, here, :] = now[field]
        for field in range(fields):
            for place in range(count):
                final[field, pl.ds(low, deep), pl.ds(place * LANES, LANES)] = solved[
                    field, pl.ds(low * count + place, deep, stride=count), :
                ]
        copies.append(
            pltpu.make_async_copy(
                final.at[:, pl.ds(low, deep), :], out.at[:, pl.ds(low, deep), :], out_sem.at[low // SUB]
            )
        )
        copies[-1].start()
    return copies


class Transport:
    def __init__(self, laid, edge, from_west_at, from_east_at, out, scratch, fields, first, count):
        self.laid, self.edge, self.out, self.fields, self.first, self.count = laid, edge, out, fields, first, count
        (
            self.from_west, self.from_east, self.here, self.there, self.speed, self.along, self.cross,
            self.halo, self.plain, self.high, self.raw, self.edges, self.sem, self.fetched, self.stored,
        ) = scratch
        self.per = laid.shape[0] // (fields + 2)
        self.size = out.shape[0] // (fields * self.per)
        self.rows = out.shape[1]
        self.wide = laid.shape[2]
        self.across = self.wide // SUB
        self.smalls = [
            pltpu.make_async_copy(from_west_at, self.from_west, self.sem.at[0]),
            pltpu.make_async_copy(from_east_at, self.from_east, self.sem.at[1]),
        ]

    @staticmethod
    def scratch(laid_shape, message_shape, out_rows, size, fields, count):
        groups, _, wide, _ = laid_shape
        return [
            pltpu.VMEM(message_shape, BF16),
            pltpu.VMEM(message_shape, BF16),
            pltpu.VMEM((fields * count, SUB, wide, LANES), F32),
            pltpu.VMEM((fields, SUB, wide, LANES), F32),
            pltpu.VMEM((2 * count, SUB, wide, LANES), F32),
            pltpu.VMEM((SUB + 1, wide, LANES), F32),
            pltpu.VMEM((SUB, wide, LANES), F32),
            pltpu.VMEM((2,) + message_shape, F32),
            pltpu.VMEM((fields, SUB, LANES + 2 * SUB, LANES), F32),
            pltpu.VMEM((fields, SUB * LANES, LANES), F32),
            pltpu.VMEM((fields * count * size, out_rows, LANES), F32),
            pltpu.VMEM(((fields + 2) * count, NSUB * wide, LANES), BF16),
            pltpu.SemaphoreType.DMA((2,)),
            pltpu.SemaphoreType.DMA((2, fields + 2, count)),
            pltpu.SemaphoreType.DMA((fields, count)),
        ]

    def fetch(self, array, turn):
        group = array * self.per + self.first + turn
        if array < self.fields:
            into = self.here.at[array * self.count + turn]
        else:
            into = self.speed.at[(array - self.fields) * self.count + turn]
        return [
            pltpu.make_async_copy(self.laid.at[group], into, self.fetched.at[0, array, turn]),
            pltpu.make_async_copy(
                self.edge.at[group], self.edges.at[array * self.count + turn], self.fetched.at[1, array, turn]
            ),
        ]

    def store(self, field, turn):
        start = (field * self.per + self.first + turn) * self.size
        return pltpu.make_async_copy(
            self.raw.at[pl.ds((field * self.count + turn) * self.size, self.size)],
            self.out.at[pl.ds(start, self.size)],
            self.stored.at[field, turn],
        )

    def start(self, turn):
        for array in range(self.fields + 2):
            for copy in self.fetch(array, turn):
                copy.start()
        if turn == 0:
            for copy in self.smalls:
                copy.start()

    def messages(self):
        for copy in self.smalls:
            copy.wait()
        for column in range(NSUB):
            self.halo[0, column] = self.from_west[column].astype(F32)
            self.halo[1, column] = self.from_east[column].astype(F32)

    def ready(self, turn):
        wide = self.wide
        coarse = (self.rows + 2 * NSUB) // SUB
        lane = lax.broadcasted_iota(jnp.int32, (SUB, LANES), 1) % coarse
        for array in range(self.fields + 2):
            for copy in self.fetch(array, turn):
                copy.wait()
            if array < self.fields:
                ref, at = self.here, array * self.count + turn
            else:
                ref, at = self.speed, (array - self.fields) * self.count + turn
            for part in range(0, NSUB * wide, 16):
                both = self.edges[array * self.count + turn, pl.ds(part, 16), :].astype(F32)
                for half in range(2):
                    value = both[half * SUB : (half + 1) * SUB]
                    row, step = divmod(part // SUB + half, self.across)
                    tile = pl.ds(step * SUB, SUB)
                    for fine, edge in ((row, 0), (row + NSUB, coarse - 1)):
                        ref[at, fine, tile, :] = jnp.where(lane == edge, value, ref[at, fine, tile, :])
            group = array * self.per + self.first + turn
            flat = ref.reshape(ref.shape[0] * SUB * wide, LANES)
            for side in range(2):
                for column in range(NSUB):
                    to = spot(column if side == 0 else wide - NSUB + column, self.across)
                    flat[pl.ds(at * (SUB * wide) + to, SUB, stride=wide), :] = self.halo[
                        side, column, pl.ds(group * SUB, SUB), :
                    ]

    def prepare(self, neighbour, fluxes, thin):
        fields, rows, plain = self.fields, self.rows, self.plain
        thin[...] = jnp.zeros(thin.shape, F32)
        up_rows = neighbour(-1, 0)
        down_rows = neighbour(1, 0)
        for field in range(fields):
            thin[field, pl.ds(0, NSUB), :] = up_rows[field * NSUB : (field + 1) * NSUB]
            thin[field, pl.ds(NSUB, rows), :] = fluxes[field]
            thin[field, pl.ds(NSUB + rows, NSUB), :] = down_rows[field * NSUB : (field + 1) * NSUB]
        lane = lax.broadcasted_iota(jnp.int32, (fields * NSUB, LANES), 1)
        sides = [sum(neighbour(di, dj) for di in (-1, 0, 1)) for dj in (-1, 1)]
        for fine in range(SUB):
            moved = []
            for side in sides:
                turned = side if fine == 0 else pltpu.roll(side, LANES - SUB * fine, 1)
                moved.append(jnp.where(lane < SUB, turned, 0.0))
            for field in range(fields):
                few = thin[field, pl.ds(fine, SUB, stride=SUB), :]
                stack = jnp.concatenate([few, jnp.zeros((LANES - SUB, LANES), F32)], axis=0)
                plain[field, fine, pl.ds(SUB, LANES), :] = stack.T
                plain[field, fine, pl.ds(SUB - NSUB, NSUB), :] = moved[0][field * NSUB : (field + 1) * NSUB]
                plain[field, fine, pl.ds(SUB + LANES, NSUB), :] = moved[1][field * NSUB : (field + 1) * NSUB]

    def force(self):
        for field in range(self.fields):
            for fine in range(SUB):
                for step in range(self.across):
                    at = (field * self.count, fine, pl.ds(step * SUB, SUB))
                    self.here[at] = (
                        self.here[at]
                        - self.plain[field, fine, pl.ds(SUB - NSUB + step, SUB, stride=self.across), :]
                    )

    def faces(self, turn):
        speed, along, cross, across = self.speed, self.along, self.cross, self.across
        for step in range(across):
            at = pl.ds(step * SUB, SUB)
            after = pl.ds(step * SUB + SUB, SUB) if step < across - 1 else pl.ds(1, SUB)
            rows_here = [speed[turn, fine, at, :] for fine in range(SUB)]
            rows_here.append(pltpu.roll(rows_here[0], LANES - 1, 1))
            for fine in range(SUB):
                face = 0.5 * (rows_here[fine] + rows_here[fine + 1])
                along[fine + 1, at, :] = face
                if fine == SUB - 1:
                    along[0, at, :] = pltpu.roll(face, 1, 1)
                lead = (self.count + turn, fine)
                cross[fine, at, :] = 0.5 * (speed[lead + (at,)] + speed[lead + (after,)])

    def update(self, src, src_at, dst, dst_at, last_step=False):
        along, cross, fields, across, wide = self.along, self.cross, self.fields, self.across, self.wide
        last = pl.ds(wide - SUB - 1, SUB)
        first = pl.ds(0, SUB)
        now = [[src[src_at[f], fine, first, :] for fine in range(SUB)] for f in range(fields)]
        carried = [[None] * SUB for _ in range(fields)]
        for fine in range(SUB):
            face = cross[fine, last, :]
            for f in range(fields):
                before = src[src_at[f], fine, last, :]
                carried[f][fine] = face * jnp.where(face > 0.0, before, now[f][fine])
        for step in range(across):
            at = pl.ds(step * SUB, SUB)
            after = pl.ds(step * SUB + SUB, SUB) if step < across - 1 else pl.ds(1, SUB)
            flow = []
            wrap = []
            face = along[0, at, :]
            for f in range(fields):
                above = pltpu.roll(now[f][SUB - 1], 1, 1)
                wrap.append(pltpu.roll(now[f][0], LANES - 1, 1))
                flow.append(face * jnp.where(face > 0.0, above, now[f][0]))
            for fine in range(SUB):
                down_face = along[fine + 1, at, :]
                side_face = cross[fine, at, :]
                down_pick = down_face > 0.0
                side_pick = side_face > 0.0
                for f in range(fields):
                    value = now[f][fine]
                    lower = now[f][fine + 1] if fine < SUB - 1 else wrap[f]
                    right = src[src_at[f], fine, after, :]
                    down_flow = down_face * jnp.where(down_pick, value, lower)
                    side_flow = side_face * jnp.where(side_pick, value, right)
                    to = pl.ds(SUB - NSUB + step, SUB, stride=across) if last_step else at
                    dst[dst_at[f], fine, to, :] = (
                        value + (flow[f] - down_flow) + (carried[f][fine] - side_flow)
                    )
                    flow[f] = down_flow
                    carried[f][fine] = side_flow
                    now[f][fine] = right

    def run(self, turn):
        fields, across, plain = self.fields, self.across, self.plain
        tall = self.rows + 2 * NSUB
        self.faces(turn)
        mine = [field * self.count + turn for field in range(fields)]
        spare = list(range(fields))

        def pair(number, carry):
            self.update(self.here, mine, self.there, spare)

            @pl.when(number < NSUB // 2 - 1)
            def _():
                self.update(self.there, spare, self.here, mine)

            @pl.when(number == NSUB // 2 - 1)
            def _():
                self.update(self.there, spare, plain, spare, last_step=True)

            return carry

        lax.fori_loop(0, NSUB // 2, pair, 0)
        for field in range(fields):
            lead = field * self.count + turn
            for fine in range(SUB):
                self.high[field, pl.ds(fine, LANES, stride=SUB), :] = plain[
                    field, fine, pl.ds(SUB, LANES), :
                ].T
            base = lead * self.size
            for level in range(self.size):
                self.raw[base + level] = self.high[field, pl.ds(level * tall + NSUB, self.rows), :]
            self.store(field, turn).start()

    def finish(self):
        for field in range(self.fields):
            for turn in range(self.count):
                self.store(field, turn).wait()


def up_kernel(
    answered_at, slots, blocks, weight, coef_c, coef_g, recip,
    out, arrived, answered, slot, block, held, made_c, made_g, made_r, sums, solved, final, sem, out_sem, *, parts
):
    share = held.shape[0] // parts
    first = [
        pltpu.make_async_copy(answered_at, arrived, sem.at[0]),
        pltpu.make_async_copy(slots, slot, sem.at[1]),
        pltpu.make_async_copy(blocks, block, sem.at[2]),
    ]
    weights = [
        pltpu.make_async_copy(
            weight.at[pl.ds(part * share, share)], held.at[pl.ds(part * share, share)], sem.at[6 + part]
        )
        for part in range(parts)
    ]
    later = [
        pltpu.make_async_copy(recip, made_r, sem.at[5]),
        pltpu.make_async_copy(coef_g, made_g, sem.at[4]),
        pltpu.make_async_copy(coef_c, made_c, sem.at[3]),
    ]
    for copy in first + weights + later:
        copy.start()
    leaving = up_part(
        arrived, answered, out, slot, block, held, made_c, made_g, made_r, sums, solved, final,
        first, weights, later, out_sem,
    )
    for copy in leaving:
        copy.wait()


def up(answered, slots, blocks, weight, coef_c, coef_g, recip, levels, cap, owners):
    fields = coef_g.shape[0]
    count = recip.shape[0]
    rows = cap * (fields + 1)
    padded = round_up(levels, SUB)
    parts = 4
    return pl.pallas_call(
        functools.partial(up_kernel, parts=parts),
        out_shape=shape((fields, levels, count * LANES)),
        in_specs=[ANY] * 7,
        out_specs=ANY,
        scratch_shapes=[
            pltpu.VMEM(answered.shape, BF16),
            pltpu.VMEM((owners, answered.shape[0] // owners, LANES), F32),
            pltpu.SMEM(slots.shape, jnp.int32),
            pltpu.SMEM(blocks.shape, jnp.int32),
            pltpu.VMEM(weight.shape, BF16),
            pltpu.VMEM(coef_c.shape, F32),
            pltpu.VMEM(coef_g.shape, F32),
            pltpu.VMEM(recip.shape, F32),
            pltpu.VMEM((count, rows, LANES), F32),
            pltpu.VMEM((fields, levels * count, LANES), F32),
            pltpu.VMEM((fields, padded, count * LANES), F32),
            pltpu.SemaphoreType.DMA((6 + parts,)),
            pltpu.SemaphoreType.DMA((padded // SUB,)),
        ],
        compiler_params=params(GRANT),
        cost_estimate=cost(1e7, 6e6),
        name="up_sweep",
    )(answered, slots, blocks, weight, coef_c, coef_g, recip)


def advect_kernel(
    laid, edge, from_west, from_east, fluxes_at, answered_at, out, arrived, answered, fluxes, thin, sem, *scratch,
    fields, atm, ocn
):
    per = laid.shape[0] // (fields + 2)
    ocean = Transport(laid, edge, from_west, from_east, out, scratch, fields, 0, per)
    smalls = [
        pltpu.make_async_copy(answered_at, arrived, sem.at[0]),
        pltpu.make_async_copy(fluxes_at, fluxes, sem.at[1]),
    ]
    ocean.start(0)
    for copy in smalls:
        copy.start()
    i = lax.axis_index("atm")
    j = lax.axis_index("ocn")

    def neighbour(di, dj):
        inside = (i + di >= 0) & (i + di < atm) & (j + dj >= 0) & (j + dj < ocn)
        index = jnp.where(inside, (i + di) * ocn + j + dj, 0)
        value = answered[index]
        width = fields + 1
        back = answered.shape[1] - extra_rows(fields)
        spare = [value[row : row + 1] for row in range(width - 1, back, width)]
        value = jnp.concatenate([value[back:]] + spare, axis=0)
        return jnp.where(inside, value, 0.0)

    for copy in smalls:
        copy.wait()
    widen(arrived, answered)
    ocean.prepare(neighbour, fluxes, thin)
    ocean.messages()
    ocean.ready(0)
    for turn in range(1, per):
        ocean.start(turn)
    ocean.force()

    def body(turn, carry):
        ocean.run(turn)
        for later in range(1, per):
            pl.when(turn == later - 1)(functools.partial(ocean.ready, later))
        return carry

    lax.fori_loop(0, per, body, 0)
    ocean.finish()


def advect(laid, edge, from_west, from_east, fluxes, answered, rows, size, atm, ocn):
    fields = fluxes.shape[0]
    per = laid.shape[0] // (fields + 2)
    return pl.pallas_call(
        functools.partial(advect_kernel, fields=fields, atm=atm, ocn=ocn),
        out_shape=shape((fields * per * size, rows, LANES)),
        in_specs=[ANY] * 6,
        out_specs=ANY,
        scratch_shapes=[
            pltpu.VMEM(answered.shape, BF16),
            pltpu.VMEM((atm * ocn, answered.shape[0] // (atm * ocn), LANES), F32),
            pltpu.VMEM(fluxes.shape, F32),
            pltpu.VMEM((fields, SUB * SUB, LANES), F32),
            pltpu.SemaphoreType.DMA((2,)),
        ]
        + Transport.scratch(laid.shape, from_west.shape, rows, size, fields, per),
        compiler_params=params(GRANT),
        cost_estimate=cost(5e7, 1.2e7),
        name="advect",
    )(laid, edge, from_west, from_east, fluxes, answered)


def per_device(
    atm_state,
    diffusivity,
    send_slot,
    atm_block,
    recv_row,
    remap_weight,
    ocean_tracer,
    ocean_velocity,
    exchange_coef,
    surface_kind,
    ice_surface,
):
    atm, ocn = lax.axis_size("atm"), lax.axis_size("ocn")
    owners = atm * ocn
    fields, levels, _ = atm_state.shape
    cap = recv_row.shape[1] // owners
    depth, rows, columns = ocean_tracer.shape[1:]
    most = LANES // ((rows + 2 * NSUB) // SUB)
    size = max(count for count in range(1, most + 1) if depth % count == 0)
    tracer = ocean_tracer.reshape(-1, rows, columns)
    speed = ocean_velocity.reshape(-1, rows, columns)

    def neighbours(axis):
        count = lax.axis_size(axis)
        up = [(place, place + 1) for place in range(count - 1)]
        return up, [(target, source) for source, target in up]

    forward, backward = neighbours("atm")
    coef_c, coef_g, recip, outgoing, first, last = down(
        atm_state, diffusivity, send_slot, atm_block, remap_weight, tracer, speed, owners, cap
    )
    south = lax.ppermute(first, "atm", backward)
    north = lax.ppermute(last, "atm", forward)
    arrived = lax.all_to_all(outgoing, ("atm", "ocn"), split_axis=0, concat_axis=0, tiled=True)
    laid, own_west, own_east = relayout(tracer, speed, size)
    fluxes, answer = flux_step(
        arrived.reshape(-1, LANES), recv_row, exchange_coef, surface_kind, ice_surface,
        ocean_tracer, own_west, north, owners, atm, ocn,
    )
    answered = lax.all_to_all(answer, ("atm", "ocn"), split_axis=0, concat_axis=0, tiled=True)
    edge, to_west, to_east = halos(north, south, own_west, own_east, laid.shape[0], size, rows)
    forward, backward = neighbours("ocn")
    from_east = lax.ppermute(to_west, "ocn", backward)
    from_west = lax.ppermute(to_east, "ocn", forward)
    atm_new = up(
        answered, send_slot, atm_block, remap_weight, coef_c, coef_g, recip, levels, cap, owners
    )
    ocean_new = advect(
        laid, edge, from_west, from_east, fluxes, answered, rows, size, atm, ocn
    )
    return atm_new, ocean_new.reshape(ocean_tracer.shape)


def solution(mesh):
    placed = (
        P(None, None, ("atm", "ocn")),
        P(None, ("atm", "ocn")),
        P(("atm", "ocn"), None),
        P(("atm", "ocn"), None),
        P(("atm", "ocn"), None),
        P(("atm", "ocn"), None, None),
        P(None, None, "atm", "ocn"),
        P(None, None, "atm", "ocn"),
        P("atm", "ocn"),
        P("atm", "ocn"),
        P(None, "atm", "ocn"),
    )
    return jax.shard_map(
        per_device,
        mesh=mesh,
        in_specs=placed,
        out_specs=(P(None, None, ("atm", "ocn")), P(None, None, "atm", "ocn")),
        check_vma=False,
    )
```
